32 devices in a mesh: ctx: 4 (over y, x), dp: 8 (over z, core).
Axes of the slice: x: 2, y: 2, z: 4, core: 2. Of those that a mesh axis runs over, the one named last changes fastest.
Arguments:
- queries: bfloat16 [8, 512, 2048], P('dp', 'ctx'), may hold values from -8 to 8
- key_rows: bfloat16 [8, 512, 256], P('dp', 'ctx'), may hold values from -8 to 8
- value_rows: bfloat16 [8, 512, 256], P('dp', 'ctx'), may hold values from -6 to 6
- stream: bfloat16 [8, 512, 2048], P('dp', 'ctx'), may hold values from -6 to 6
- norm_gain: float32 [2048], replicated, may hold values from 0.1 to 1.9
- expert_ids: int32 [8, 512, 8], P('dp', 'ctx'), may hold values from 0 to 127, all different within a row; in each aligned block of 128 rows (0 to 127, 128 to 255, ..., all dimensions but the last counted through in order) at most 12 rows name the same one
- gate_values: float32 [8, 512, 8], P('dp', 'ctx'), may hold values from 0.1 to 1
- w_gate: bfloat16 [8, 2048, 384], P('dp', 'ctx'), may hold values from -0.125 to 0.125
- w_up: bfloat16 [8, 2048, 384], P('dp', 'ctx'), may hold values from -0.125 to 0.125
- w_down: bfloat16 [8, 384, 2048], P('dp', None, 'ctx'), may hold values from -0.3125 to 0.3125
Outputs:
- attended: bfloat16 [8, 512, 2048], P('dp', 'ctx')
- expert_out: bfloat16 [8, 512, 2048], P('dp', 'ctx')
The draws below stay inside these ranges and needn't reach their ends.
Inputs may be any that keep to these rules, and one draw needn't show every extreme that they name: `expert_ids`: among the rows of one device, no expert is chosen by more than 12 rows; some expert reaches 12.
All inputs are finite; a program needn't handle non-finite values.
Results may differ from the reference program's by a relative error of at most 0.012.
Values may be sent and summed in bfloat16 or wider, within the bound.
A program may use at most 64 MiB of HBM per device.

```python
import math
import jax
import jax.numpy as jnp
import numpy as np
from jax import lax

D = 2048
HD = 128
EXPERTS = 128
TOP = 8
QH = 16
KVH = 2
EXP_HID = 384
TOK_DEV = 128
LENGTH = 512
SEQS = 8
FLIGHT = 8
CAP = 12
N_CTX = 4


def paired_fields(key):
    query_key = jax.random.fold_in(key, 11)
    other_key = jax.random.fold_in(key, 23)
    queries = jnp.clip(jax.random.normal(query_key, (SEQS, LENGTH, QH * HD), jnp.float32), -4.0, 4.0)
    keyset = jnp.clip(jax.random.normal(other_key, (SEQS, LENGTH, KVH * HD), jnp.float32), -4.0, 4.0)
    return (queries, keyset)


def draw_queries(key, part):
    return paired_fields(key)[0].astype(jnp.bfloat16)


def draw_key_rows(key, part):
    return paired_fields(key)[1].astype(jnp.bfloat16)


def block_scale(key, extent, shards, least, high):
    def one(dim, blocks):
        draws = jax.random.uniform(jax.random.fold_in(jax.random.fold_in(key, 6), dim), (blocks,), jnp.float32, least / len(shards), high / len(shards))
        return jnp.repeat(jnp.exp(draws), extent[dim] // blocks).reshape((-1,) + (1,) * (len(extent) - dim - 1))

    loudness = one(*shards[0])
    for cut in shards[1:]:
        loudness = loudness * one(*cut)
    return loudness


def routed_block(rng, own, number, rows, amount, top, most, lean):
    sequence = jax.random.permutation(rng, amount)
    heavy_load, usual = load_shares(amount, rows * top, most, lean, True), load_shares(amount, rows * top, most, lean, False)
    places = jnp.arange(amount)

    def named(lengths, offset_by):
        used = int((lengths > 0).sum())
        fixed = max(1, used // 4)
        passed = fixed + (places - fixed + offset_by * (used - fixed)) % max(1, amount - fixed)
        return jnp.zeros((amount,), jnp.int32).at[sequence[jnp.where(places < fixed, places, passed)]].set(jnp.asarray(lengths, jnp.int32))

    lengths = jnp.where(number % 4 == 0, named(heavy_load, number // 4), named(usual, number - number // 4 - 1))
    mixed = jax.random.permutation(jax.random.fold_in(own, 3), amount)
    giver, receiver = mixed[0:amount // 2 * 2:2], mixed[1:amount // 2 * 2:2]
    margin = jnp.minimum(lengths[giver] - 1, most - lengths[receiver]) // 2
    margin = jnp.where((giver == sequence[0]) | (receiver == sequence[0]) | (lengths[receiver] == 0), 0, jnp.maximum(margin, 0))
    passed = jax.random.randint(jax.random.fold_in(own, 4), (amount // 2,), 0, 1 << 20) % (margin + 1)
    lengths = lengths.at[giver].add(-passed).at[receiver].add(passed)
    members = jnp.searchsorted(jnp.cumsum(lengths), jnp.arange(rows * top), side="right").astype(jnp.int32)
    table = members.reshape(top, rows).T
    table = table[jax.random.permutation(jax.random.fold_in(own, 1), rows)]
    offset_by = jax.random.randint(jax.random.fold_in(own, 2), (rows, 1), 0, top)
    return jnp.take_along_axis(table, (jnp.arange(top)[None, :] + offset_by) % top, axis=1)


def load_shares(number_of, total, most, skew, full):
    loads = [(1 << 20) // math.isqrt(grade ** skew) + 1 for grade in range(1, number_of + 1)]
    largest = most if full else min(most, max(-(-total // number_of), total * loads[0] // sum(loads)))
    least = 1 if total - largest >= number_of - 1 else 0
    given, spare = [largest] + [least] * (number_of - 1), total - largest - least * (number_of - 1)
    while spare > 0:
        free = [i for i in range(1, number_of) if given[i] < largest] or [i for i in range(1, number_of) if given[i] < most]
        mass, budget = sum([loads[i] for i in free]), spare
        for i in free:
            addition = min(most - given[i], max(1, budget * loads[i] // mass), spare)
            given[i] = given[i] + addition
            spare = spare - addition
    return np.array(given)


def bell_draw(stream_key, dims, deviation, reach, split=(), held_as=jnp.bfloat16):
    array = deviation * jax.random.normal(stream_key, dims, jnp.float32)
    if split:
        array = array * block_scale(stream_key, dims, split, -0.22, 0.18)
    return jnp.clip(array, -reach, reach).astype(held_as)


def setup_inputs(seed: int = 0) -> dict:
    splits = jax.random.split(jax.random.key(seed), 11)
    queries = draw_queries(jax.random.fold_in(splits[10], 71), 0)
    key_rows = draw_key_rows(jax.random.fold_in(splits[10], 71), 0)
    value_rows = bell_draw(splits[2], (SEQS, LENGTH, KVH * HD), 1.0, 6.0, ((0, 8), (1, 4)))
    stream = bell_draw(splits[3], (SEQS, LENGTH, D), 1.0, 6.0, ((0, 8), (1, 4)))
    norm_gain = jnp.clip(1.0 + 0.18 * jax.random.normal(splits[4], (D,), jnp.float32), 0.1, 1.9)
    expert_ids_keys = jax.random.split(jax.random.fold_in(splits[5], 1), SEQS * LENGTH // TOK_DEV)
    expert_ids_turns = jax.random.permutation(jax.random.fold_in(splits[5], 3), SEQS * LENGTH // TOK_DEV)
    expert_ids = jax.vmap(lambda own, number: routed_block(jax.random.fold_in(splits[5], 2), own, number, TOK_DEV, EXPERTS, TOP, CAP, 1))(expert_ids_keys, expert_ids_turns).reshape((SEQS, LENGTH, TOP))
    gate_values = jnp.clip(jnp.exp(math.log(1.0) - 2.3025851 * jax.random.uniform(splits[6], (SEQS, LENGTH, TOP), jnp.float32) ** block_scale(splits[6], (SEQS, LENGTH, TOP), ((0, 8), (1, 4)), -0.2, 0.2)), 0.1, 1.0)
    w_gate = bell_draw(splits[7], (FLIGHT, D, EXP_HID), D ** -0.5, 0.125, ((0, 8), (1, 4)))
    w_up = bell_draw(splits[8], (FLIGHT, D, EXP_HID), D ** -0.5, 0.125, ((0, 8), (1, 4)))
    w_down = bell_draw(splits[9], (FLIGHT, EXP_HID, D), EXP_HID ** -0.5, 0.3125, ((0, 8), (2, 4)))
    return {"queries": queries, "key_rows": key_rows, "value_rows": value_rows, "stream": stream, "norm_gain": norm_gain, "expert_ids": expert_ids, "gate_values": gate_values, "w_gate": w_gate, "w_up": w_up, "w_down": w_down}


def attend_sequence(operands):
    query_seq, key_seq, value_seq = operands
    group = QH // KVH
    scale = 1.0 / math.sqrt(HD)
    positions = jnp.arange(LENGTH, dtype=jnp.int32)
    allowed = positions[None, :] <= positions[:, None]
    query_heads = query_seq.reshape(LENGTH, KVH, group, HD)
    key_heads = key_seq.reshape(LENGTH, KVH, HD)
    value_heads = value_seq.reshape(LENGTH, KVH, HD)

    def one_head(head):
        query_group = query_heads[:, head].astype(jnp.float32)
        key_group = key_heads[:, head].astype(jnp.float32)
        value_group = value_heads[:, head].astype(jnp.float32)
        scores = jnp.einsum('qgd,kd->gqk', query_group, key_group) * scale
        masked = jnp.where(allowed[None], scores, -jnp.inf)
        largest = lax.optimization_barrier(jnp.max(masked, axis=-1, keepdims=True))
        probs = jnp.where(allowed[None], jnp.exp(scores - largest), 0.0)
        total = lax.optimization_barrier(jnp.sum(probs, axis=-1))
        rounded = probs.astype(jnp.bfloat16).astype(jnp.float32)
        mixed = jnp.einsum('gqk,kd->gqd', rounded, value_group)
        return mixed / total[..., None]
    heads_out = lax.map(one_head, jnp.arange(KVH, dtype=jnp.int32))
    return heads_out.transpose(2, 0, 1, 3).reshape(LENGTH, QH * HD).astype(jnp.bfloat16)

def reference(queries, key_rows, value_rows, stream, norm_gain, expert_ids, gate_values, w_gate, w_up, w_down):
    attended = lax.map(attend_sequence, (queries, key_rows, value_rows))
    count = SEQS * LENGTH
    flat = stream.reshape(count, D).astype(jnp.float32)
    normed = (flat * lax.rsqrt(lax.optimization_barrier(jnp.mean(flat * flat, axis=-1, keepdims=True)) + 1e-06) * norm_gain.astype(jnp.float32)).astype(jnp.bfloat16)
    chosen_ids = expert_ids.reshape(count, TOP)
    gates = gate_values.reshape(count, TOP)
    most_rows = SEQS * N_CTX * CAP

    def expert_step(total, index):
        hits = chosen_ids == index
        weight = lax.optimization_barrier(jnp.sum(jnp.where(hits, gates, 0.0), axis=1))
        chosen = jnp.any(hits, axis=1)
        rows = jnp.nonzero(chosen, size=most_rows, fill_value=0)[0].astype(jnp.int32)
        live = jnp.arange(most_rows, dtype=jnp.int32) < jnp.sum(chosen.astype(jnp.int32))
        picked = normed[rows]
        gate = jnp.dot(picked, w_gate[index], preferred_element_type=jnp.float32)
        upper = jnp.dot(picked, w_up[index], preferred_element_type=jnp.float32)
        hidden = (jax.nn.silu(gate) * upper).astype(jnp.bfloat16)
        answer = jnp.dot(hidden, w_down[index], preferred_element_type=jnp.float32).astype(jnp.bfloat16)
        scaled = answer.astype(jnp.float32) * jnp.where(live, weight[rows], 0.0)[:, None]
        return (total.at[rows].add(scaled), None)
    start_total = jnp.zeros((count, D), jnp.float32)
    total, unused = lax.scan(expert_step, start_total, jnp.arange(FLIGHT, dtype=jnp.int32))
    expert_out = total.astype(jnp.bfloat16).reshape(SEQS, LENGTH, D)
    return (attended, expert_out)
```

```python
import functools
import math

import jax
import jax.numpy as jnp
from jax import lax
from jax.experimental import pallas as pl
from jax.experimental.pallas import tpu as pltpu
from jax.sharding import PartitionSpec as P

HD = 128
SLOT = 16
MESH = pl.DeviceIdType.MESH
hidden_score = -1e30


def fused(
    n_ctx, n_dp, split,
    q_ref, k_ref, v_ref, s_ref, gain_ref, ids_ref, gv_ref, wg_ref, wu_ref, wd_ref,
    att_ref, out_ref,
    outgoing, arrived, kbuf, vbuf, rs_out, rs_in, own, hid, answers, ret, w_hi, w_lo,
    k_send, k_recv, v_send, v_recv, a_send, a_recv, p_send, p_recv, h_send, h_recv,
    r_send, r_recv,
):
    my_c = lax.axis_index("ctx")
    my_d = lax.axis_index("dp")
    me = my_c * n_dp + my_d
    total = n_ctx * n_dp
    tokens, width = s_ref.shape[1], s_ref.shape[2]
    slots = n_dp * SLOT
    col = width // n_ctx
    units = wg_ref.shape[2]
    heads = q_ref.shape[2] // HD
    kv_heads = k_ref.shape[2] // HD
    group = heads // kv_heads

    barrier = pltpu.get_barrier_semaphore()

    def greet(i, carry):
        peer = lax.rem(me + i, total)
        pl.semaphore_signal(
            barrier, inc=1, device_id=(peer // n_dp, lax.rem(peer, n_dp)), device_id_type=MESH
        )
        return carry

    lax.fori_loop(1, total, greet, 0)

    lane = lax.broadcasted_iota(jnp.int32, (tokens, slots), 1)
    expert = lane // SLOT
    hot = jnp.zeros((tokens, slots), jnp.float32)
    weight = jnp.zeros((tokens, slots), jnp.float32)
    ids = ids_ref[0]
    gates = gv_ref[0]
    for t in range(ids_ref.shape[2]):
        hit = ids[:, t : t + 1] == expert
        hot = hot + jnp.where(hit, 1.0, 0.0)
        weight = weight + jnp.where(hit, gates[:, t : t + 1], 0.0)
    rows_i = lax.broadcasted_iota(jnp.int32, (tokens, tokens), 0)
    cols_i = lax.broadcasted_iota(jnp.int32, (tokens, tokens), 1)
    before = jnp.where(cols_i < rows_i, 1.0, 0.0).astype(jnp.bfloat16)
    rank = jnp.dot(before, hot.astype(jnp.bfloat16), preferred_element_type=jnp.float32)
    place = jnp.where(rank == (lane % SLOT).astype(jnp.float32), hot, 0.0)
    weighted = place * weight
    upper = weighted.astype(jnp.bfloat16)
    w_hi[...] = upper
    w_lo[...] = (weighted - upper.astype(jnp.float32)).astype(jnp.bfloat16)
    select = place.T.astype(jnp.bfloat16)

    pl.semaphore_wait(barrier, total - 1)

    def ctx_copy(src, dst, send, recv, c):
        return pltpu.make_async_remote_copy(
            src_ref=src, dst_ref=dst, send_sem=send, recv_sem=recv,
            device_id=(c, my_d), device_id_type=MESH,
        )

    others = [lax.rem(my_c + i, n_ctx) for i in range(1, n_ctx)]
    for c in others:
        ctx_copy(k_ref.at[0], kbuf.at[my_c], k_send.at[c], k_recv.at[my_c], c).start()
        ctx_copy(v_ref.at[0], vbuf.at[my_c], v_send.at[c], v_recv.at[my_c], c).start()

    x = s_ref[0].astype(jnp.float32)
    normed = (
        x * lax.rsqrt(jnp.mean(x * x, axis=-1, keepdims=True) + 1e-06) * gain_ref[...]
    ).astype(jnp.bfloat16)
    for c in range(n_ctx):
        outgoing[c] = jnp.dot(
            select, normed[:, c * col : (c + 1) * col], preferred_element_type=jnp.float32
        ).astype(jnp.bfloat16)

    my_rows = pl.ds(pl.multiple_of(my_d * SLOT, SLOT), SLOT)

    def scatter(src, dst, send, recv, c, first):
        def one(i, carry):
            d = lax.rem(my_d + i, n_dp)
            pltpu.make_async_remote_copy(
                src_ref=src.at[c, pl.ds(pl.multiple_of(d * SLOT, SLOT), SLOT)],
                dst_ref=dst.at[my_c, my_rows],
                send_sem=send.at[c],
                recv_sem=recv.at[my_c],
                device_id=(c, d),
                device_id_type=MESH,
            ).start()
            return carry

        lax.fori_loop(first, n_dp, one, 0)

    def group_of(buf, send, recv, c, rows):
        part = buf.at[c, pl.ds(0, rows)]
        return pltpu.make_async_remote_copy(
            src_ref=part, dst_ref=part, send_sem=send.at[c], recv_sem=recv.at[c],
            device_id=(c, lax.rem(my_d + 1, n_dp)), device_id_type=MESH,
        )

    for c in others:
        scatter(outgoing, arrived, a_send, a_recv, c, 0)
    scatter(outgoing, arrived, a_send, a_recv, my_c, 1)
    arrived[my_c, my_rows] = outgoing[my_c, my_rows]
    kbuf[my_c] = k_ref[0]
    vbuf[my_c] = v_ref[0]
    for c in others:
        ctx_copy(k_ref.at[0], kbuf.at[c], k_send.at[c], k_recv.at[c], c).wait_recv()
        ctx_copy(v_ref.at[0], vbuf.at[c], v_send.at[c], v_recv.at[c], c).wait_recv()

    keys = n_ctx * tokens
    scale = 1.0 / math.sqrt(HD)

    def attend(first, last):
        def one(h, carry):
            at = pl.ds(pl.multiple_of(h * HD, HD), HD)
            kv_at = pl.ds(pl.multiple_of((h // group) * HD, HD), HD)
            k_all = kbuf[:, :, kv_at].reshape(keys, HD)
            v_all = vbuf[:, :, kv_at].reshape(keys, HD)
            scores = lax.dot_general(
                q_ref[0, :, at], k_all, (((1,), (1,)), ((), ())),
                preferred_element_type=jnp.float32,
            ) * scale
            q_pos = my_c * tokens + lax.broadcasted_iota(jnp.int32, (tokens, keys), 0)
            k_pos = lax.broadcasted_iota(jnp.int32, (tokens, keys), 1)
            scores = jnp.where(k_pos <= q_pos, scores, hidden_score)
            probs = jnp.exp(scores - jnp.max(scores, axis=-1, keepdims=True))
            mass = jnp.sum(probs, axis=-1, keepdims=True)
            mixed = jnp.dot(probs.astype(jnp.bfloat16), v_all, preferred_element_type=jnp.float32)
            att_ref[0, :, at] = (mixed / mass).astype(jnp.bfloat16)
            return carry

        lax.fori_loop(first, last, one, 0)

    marks = [0] + [heads * s // 16 for s in split] + [heads]
    attend(marks[0], marks[1])

    for c in others:
        group_of(arrived, a_send, a_recv, c, slots).wait_recv()
        rows = arrived[c]
        rs_out[c, :, :units] = jnp.dot(
            rows, wg_ref[0], preferred_element_type=jnp.float32
        ).astype(jnp.bfloat16)
        rs_out[c, :, units:] = jnp.dot(
            rows, wu_ref[0], preferred_element_type=jnp.float32
        ).astype(jnp.bfloat16)
        ctx_copy(rs_out.at[c], rs_in.at[my_c], p_send.at[c], p_recv.at[my_c], c).start()
    group_of(arrived, a_send, a_recv, my_c, slots - SLOT).wait_recv()
    rows = arrived[my_c]
    own[:, :units] = jnp.dot(rows, wg_ref[0], preferred_element_type=jnp.float32)
    own[:, units:] = jnp.dot(rows, wu_ref[0], preferred_element_type=jnp.float32)
    attend(marks[1], marks[2])
    for c in others:
        ctx_copy(rs_out.at[c], rs_in.at[c], p_send.at[c], p_recv.at[c], c).wait_recv()
    sums = own[...]
    for c in others:
        sums = sums + rs_in[c].astype(jnp.float32)
    gate = sums[:, :units]
    hid[my_c] = (gate / (1.0 + jnp.exp(-gate)) * sums[:, units:]).astype(jnp.bfloat16)
    for c in others:
        ctx_copy(hid.at[my_c], hid.at[my_c], h_send.at[c], h_recv.at[my_c], c).start()

    def answer(c):
        answers[c] = jnp.dot(hid[c], wd_ref[0], preferred_element_type=jnp.float32).astype(
            jnp.bfloat16
        )

    answer(my_c)
    scatter(answers, ret, r_send, r_recv, my_c, 1)
    ret[my_c, my_rows] = answers[my_c, my_rows]
    attend(marks[2], marks[3])
    for c in others:
        ctx_copy(hid.at[my_c], hid.at[c], h_send.at[c], h_recv.at[c], c).wait_recv()
        answer(c)
        scatter(answers, ret, r_send, r_recv, c, 0)
    attend(marks[3], marks[4])

    def combine(c):
        part = ret[c]
        mixed = jnp.dot(w_hi[...], part, preferred_element_type=jnp.float32) + jnp.dot(
            w_lo[...], part, preferred_element_type=jnp.float32
        )
        out_ref[0, :, pl.ds(pl.multiple_of(c * col, col), col)] = mixed.astype(jnp.bfloat16)

    group_of(ret, r_send, r_recv, my_c, slots - SLOT).wait_recv()
    combine(my_c)
    for c in others:
        group_of(ret, r_send, r_recv, c, slots).wait_recv()
        combine(c)

    group_of(outgoing, a_send, a_recv, my_c, slots - SLOT).wait_send()
    group_of(answers, r_send, r_recv, my_c, slots - SLOT).wait_send()
    for c in others:
        ctx_copy(k_ref.at[0], kbuf.at[c], k_send.at[c], k_recv.at[c], c).wait_send()
        ctx_copy(v_ref.at[0], vbuf.at[c], v_send.at[c], v_recv.at[c], c).wait_send()
        group_of(outgoing, a_send, a_recv, c, slots).wait_send()
        ctx_copy(rs_out.at[c], rs_in.at[c], p_send.at[c], p_recv.at[c], c).wait_send()
        ctx_copy(hid.at[my_c], hid.at[c], h_send.at[c], h_recv.at[c], c).wait_send()
        group_of(answers, r_send, r_recv, c, slots).wait_send()


def shards(n_ctx, n_dp, queries, key_rows, value_rows, stream, norm_gain, *rest):
    tokens, width = stream.shape[1:]
    kv = key_rows.shape[2]
    units = rest[2].shape[2]
    slots = n_dp * SLOT
    col = width // n_ctx
    bf16, f32 = jnp.bfloat16, jnp.float32
    scratch = [
        ((n_ctx, slots, col), bf16),
        ((n_ctx, slots, col), bf16),
        ((n_ctx, tokens, kv), bf16),
        ((n_ctx, tokens, kv), bf16),
        ((n_ctx, slots, 2 * units), bf16),
        ((n_ctx, slots, 2 * units), bf16),
        ((slots, 2 * units), f32),
        ((n_ctx, slots, units), bf16),
        ((n_ctx, slots, col), bf16),
        ((n_ctx, slots, col), bf16),
        ((tokens, slots), bf16),
        ((tokens, slots), bf16),
    ]
    need = sum(math.prod(s) * jnp.dtype(t).itemsize for s, t in scratch)
    vmem = pl.BlockSpec(memory_space=pltpu.VMEM)
    return pl.pallas_call(
        functools.partial(fused, n_ctx, n_dp, (8, 12, 14)),
        out_shape=(
            jax.ShapeDtypeStruct(queries.shape, bf16),
            jax.ShapeDtypeStruct(stream.shape, bf16),
        ),
        in_specs=[vmem] * 10,
        out_specs=(vmem, vmem),
        scratch_shapes=[pltpu.VMEM(s, t) for s, t in scratch]
        + [pltpu.SemaphoreType.DMA((n_ctx,))] * 12,
        compiler_params=pltpu.CompilerParams(
            collective_id=0, has_side_effects=True, vmem_limit_bytes=need + (16 << 20)
        ),
    )(queries, key_rows, value_rows, stream, norm_gain.reshape(1, width), *rest)


def solution(mesh):
    rows = P("dp", "ctx", None)
    return jax.shard_map(
        functools.partial(shards, mesh.shape["ctx"], mesh.shape["dp"]),
        mesh=mesh,
        in_specs=(rows,) * 4 + (P(),) + (rows,) * 4 + (P("dp", None, "ctx"),),
        out_specs=(rows, rows),
        check_vma=False,
    )
```

```python
import functools
import math

import jax
import jax.numpy as jnp
from jax import lax
from jax.experimental import pallas as pl
from jax.experimental.pallas import tpu as pltpu
from jax.sharding import PartitionSpec as P

HD = 128
CAP = 12
TILE = 16
LANES = 128
MESH = pl.DeviceIdType.MESH
hidden_score = -1e30


def message_form(col):
    chunks = col // LANES
    if chunks * CAP % TILE == 0:
        return CAP, chunks
    return TILE, 1


def fused(
    n_ctx, n_dp, split,
    q_hbm, k_hbm, v_hbm, s_hbm, gain_hbm, ids_hbm, gv_hbm, wg_hbm, wu_hbm, wd_hbm,
    att_ref, out_ref,
    q_ref, s_ref, gain_ref, ids_ref, gv_ref, wgu, wd_ref,
    outgoing, arrived, kbuf, vbuf, rs_out, rs_in, own, hid, answers, ret,
    w_hi, w_lo, sort, unsort,
    k_send, k_recv, v_send, v_recv, a_send, a_recv, p_send, p_recv, h_send, h_recv,
    r_send, r_recv, load_sem,
):
    my_c = lax.axis_index("ctx")
    my_d = lax.axis_index("dp")
    me = my_c * n_dp + my_d
    total = n_ctx * n_dp
    tokens, width = s_ref.shape
    col = width // n_ctx
    slot, chunks = message_form(col)
    message = slot * chunks
    wide = col // chunks
    rows_all = n_dp * slot
    lines = n_dp * message
    units = wd_ref.shape[0]
    heads = q_ref.shape[1] // HD
    kv_heads = kbuf.shape[2] // HD
    group = heads // kv_heads

    pairs = (
        (ids_hbm.at[0], ids_ref),
        (gv_hbm.at[0], gv_ref),
        (s_hbm.at[0], s_ref),
        (gain_hbm, gain_ref),
        (wg_hbm.at[0], wgu.at[:, pl.ds(0, units)]),
        (wu_hbm.at[0], wgu.at[:, pl.ds(units, units)]),
        (k_hbm.at[0], kbuf.at[my_c]),
        (v_hbm.at[0], vbuf.at[my_c]),
        (q_hbm.at[0], q_ref),
        (wd_hbm.at[0], wd_ref),
    )
    loads = [pltpu.make_async_copy(a, b, load_sem.at[i]) for i, (a, b) in enumerate(pairs)]
    for load in loads:
        load.start()

    barrier = pltpu.get_barrier_semaphore()

    def greet(i, carry):
        peer = lax.rem(me + i, total)
        pl.semaphore_signal(
            barrier, inc=1, device_id=(peer // n_dp, lax.rem(peer, n_dp)), device_id_type=MESH
        )
        return carry

    lax.fori_loop(1, total, greet, 0)

    def parts_of(line):
        rest = lax.rem(line, message)
        return lax.div(line, message), lax.div(rest, slot), lax.rem(rest, slot)

    expert, chunk, place_rank = parts_of(lax.broadcasted_iota(jnp.int32, (lines, 1), 0))
    _, chunk_lane, rank_lane = parts_of(lax.broadcasted_iota(jnp.int32, (1, lines), 1))
    expert_lane = lax.div(lax.broadcasted_iota(jnp.int32, (1, lines), 1), message)
    if chunks > 1:
        goes = chunk * rows_all + expert * slot + place_rank
        goes_lane = chunk_lane * rows_all + expert_lane * slot + rank_lane
        square = (lines, lines)
        unsort[...] = jnp.where(
            lax.broadcasted_iota(jnp.int32, square, 1) == goes, 1.0, 0.0
        ).astype(jnp.bfloat16)
        sort[...] = jnp.where(
            lax.broadcasted_iota(jnp.int32, square, 0) == goes_lane, 1.0, 0.0
        ).astype(jnp.bfloat16)
    loads[0].wait()
    loads[1].wait()
    hot = jnp.zeros((lines, tokens), jnp.float32)
    weight = jnp.zeros((lines, tokens), jnp.float32)
    for t in range(ids_ref.shape[0]):
        hit = ids_ref[t : t + 1, :] == expert
        hot = jnp.where(hit, 1.0, hot)
        weight = jnp.where(hit, gv_ref[t : t + 1, :], weight)
    rows_i = lax.broadcasted_iota(jnp.int32, (tokens, tokens), 0)
    cols_i = lax.broadcasted_iota(jnp.int32, (tokens, tokens), 1)
    before = jnp.where(rows_i < cols_i, 1.0, 0.0).astype(jnp.bfloat16)
    rank = jnp.dot(hot.astype(jnp.bfloat16), before, preferred_element_type=jnp.float32)
    place = jnp.where(rank == place_rank.astype(jnp.float32), hot, 0.0)
    select = jnp.concatenate(
        [jnp.where(chunk == j, place, 0.0).astype(jnp.bfloat16) for j in range(chunks)], axis=1
    )

    loads[2].wait()
    loads[3].wait()
    x = s_ref[...].astype(jnp.float32)
    normed = (
        x * lax.rsqrt(jnp.mean(x * x, axis=-1, keepdims=True) + 1e-06) * gain_ref[...]
    ).astype(jnp.bfloat16)
    for c in range(n_ctx):
        stacked = jnp.concatenate(
            [normed[:, c * col + j * wide : c * col + (j + 1) * wide] for j in range(chunks)], axis=0
        )
        outgoing[c] = jnp.dot(select, stacked, preferred_element_type=jnp.float32).astype(
            jnp.bfloat16
        )

    pl.semaphore_wait(barrier, total - 1)

    def ctx_copy(src, dst, send, recv, c):
        return pltpu.make_async_remote_copy(
            src_ref=src, dst_ref=dst, send_sem=send, recv_sem=recv,
            device_id=(c, my_d), device_id_type=MESH,
        )

    others = [lax.rem(my_c + i, n_ctx) for i in range(1, n_ctx)]
    my_rows = pl.ds(pl.multiple_of(my_d * message, message), message)

    def scatter(src, dst, send, recv, c, first):
        def one(i, carry):
            d = lax.rem(my_d + i, n_dp)
            pltpu.make_async_remote_copy(
                src_ref=src.at[c, pl.ds(pl.multiple_of(d * message, message), message)],
                dst_ref=dst.at[my_c, my_rows],
                send_sem=send.at[c],
                recv_sem=recv.at[my_c],
                device_id=(c, d),
                device_id_type=MESH,
            ).start()
            return carry

        lax.fori_loop(first, n_dp, one, 0)

    def group_of(buf, send, recv, c, rows):
        part = buf.at[c, pl.ds(0, rows)]
        return pltpu.make_async_remote_copy(
            src_ref=part, dst_ref=part, send_sem=send.at[c], recv_sem=recv.at[c],
            device_id=(c, lax.rem(my_d + 1, n_dp)), device_id_type=MESH,
        )

    for c in others:
        scatter(outgoing, arrived, a_send, a_recv, c, 0)
    scatter(outgoing, arrived, a_send, a_recv, my_c, 1)
    for c in others:
        ctx_copy(k_hbm.at[0], kbuf.at[my_c], k_send.at[c], k_recv.at[my_c], c).start()
        ctx_copy(v_hbm.at[0], vbuf.at[my_c], v_send.at[c], v_recv.at[my_c], c).start()
    arrived[my_c, my_rows] = outgoing[my_c, my_rows]

    back = (place * weight).T
    for j in range(chunks):
        of_chunk = jnp.where(chunk_lane == j, back, 0.0)
        upper = of_chunk.astype(jnp.bfloat16)
        w_hi[j * tokens : (j + 1) * tokens] = upper
        w_lo[j * tokens : (j + 1) * tokens] = (of_chunk - upper.astype(jnp.float32)).astype(
            jnp.bfloat16
        )

    keys = n_ctx * tokens
    scale = 1.0 / math.sqrt(HD)

    def attend(first, last):
        def one(h, carry):
            at = pl.ds(pl.multiple_of(h * HD, HD), HD)
            kv_at = pl.ds(pl.multiple_of((h // group) * HD, HD), HD)
            k_all = kbuf[:, :, kv_at].reshape(keys, HD)
            v_all = vbuf[:, :, kv_at].reshape(keys, HD)
            scores = lax.dot_general(
                q_ref[:, at], k_all, (((1,), (1,)), ((), ())),
                preferred_element_type=jnp.float32,
            ) * scale
            q_pos = my_c * tokens + lax.broadcasted_iota(jnp.int32, (tokens, keys), 0)
            k_pos = lax.broadcasted_iota(jnp.int32, (tokens, keys), 1)
            scores = jnp.where(k_pos <= q_pos, scores, hidden_score)
            probs = jnp.exp(scores - jnp.max(scores, axis=-1, keepdims=True))
            mass = jnp.sum(probs, axis=-1, keepdims=True)
            mixed = jnp.dot(probs.astype(jnp.bfloat16), v_all, preferred_element_type=jnp.float32)
            att_ref[0, :, at] = (mixed / mass).astype(jnp.bfloat16)
            return carry

        lax.fori_loop(first, last, one, 0)

    mark = heads * split // 16

    def partial(c):
        block = arrived[c]
        if chunks > 1:
            block = jnp.dot(sort[...], block, preferred_element_type=jnp.float32).astype(
                jnp.bfloat16
            )
            block = jnp.concatenate(
                [block[j * rows_all : (j + 1) * rows_all] for j in range(chunks)], axis=1
            )
        return jnp.dot(block, wgu[...], preferred_element_type=jnp.float32)

    loads[4].wait()
    loads[5].wait()
    for c in others:
        group_of(arrived, a_send, a_recv, c, lines).wait_recv()
        rs_out[c] = partial(c).astype(jnp.bfloat16)
        ctx_copy(rs_out.at[c], rs_in.at[my_c], p_send.at[c], p_recv.at[my_c], c).start()
    group_of(arrived, a_send, a_recv, my_c, lines - message).wait_recv()
    own[...] = partial(my_c)
    for load in loads[6:]:
        load.wait()
    for c in others:
        ctx_copy(k_hbm.at[0], kbuf.at[c], k_send.at[c], k_recv.at[c], c).wait_recv()
        ctx_copy(v_hbm.at[0], vbuf.at[c], v_send.at[c], v_recv.at[c], c).wait_recv()
    attend(0, mark)
    for c in others:
        ctx_copy(rs_out.at[c], rs_in.at[c], p_send.at[c], p_recv.at[c], c).wait_recv()
    sums = own[...]
    for c in others:
        sums = sums + rs_in[c].astype(jnp.float32)
    gate = sums[:, :units]
    hid[my_c] = (gate / (1.0 + jnp.exp(-gate)) * sums[:, units:]).astype(jnp.bfloat16)
    for c in others:
        ctx_copy(hid.at[my_c], hid.at[my_c], h_send.at[c], h_recv.at[my_c], c).start()

    def answer(c):
        block = jnp.dot(hid[c], wd_ref[...], preferred_element_type=jnp.float32).astype(
            jnp.bfloat16
        )
        if chunks > 1:
            block = jnp.concatenate(
                [block[:, j * wide : (j + 1) * wide] for j in range(chunks)], axis=0
            )
            block = jnp.dot(unsort[...], block, preferred_element_type=jnp.float32).astype(
                jnp.bfloat16
            )
        answers[c] = block

    answer(my_c)
    scatter(answers, ret, r_send, r_recv, my_c, 1)
    ret[my_c, my_rows] = answers[my_c, my_rows]
    for c in others:
        ctx_copy(hid.at[my_c], hid.at[c], h_send.at[c], h_recv.at[c], c).wait_recv()
        answer(c)
        scatter(answers, ret, r_send, r_recv, c, 0)
    attend(mark, heads)

    def combine(c):
        part = ret[c]
        mixed = jnp.dot(w_hi[...], part, preferred_element_type=jnp.float32) + jnp.dot(
            w_lo[...], part, preferred_element_type=jnp.float32
        )
        mixed = jnp.concatenate(
            [mixed[j * tokens : (j + 1) * tokens] for j in range(chunks)], axis=1
        )
        out_ref[0, :, pl.ds(pl.multiple_of(c * col, col), col)] = mixed.astype(jnp.bfloat16)

    group_of(ret, r_send, r_recv, my_c, lines - message).wait_recv()
    combine(my_c)
    for c in others:
        group_of(ret, r_send, r_recv, c, lines).wait_recv()
        combine(c)

    group_of(outgoing, a_send, a_recv, my_c, lines - message).wait_send()
    group_of(answers, r_send, r_recv, my_c, lines - message).wait_send()
    for c in others:
        ctx_copy(k_hbm.at[0], kbuf.at[c], k_send.at[c], k_recv.at[c], c).wait_send()
        ctx_copy(v_hbm.at[0], vbuf.at[c], v_send.at[c], v_recv.at[c], c).wait_send()
        group_of(outgoing, a_send, a_recv, c, lines).wait_send()
        ctx_copy(rs_out.at[c], rs_in.at[c], p_send.at[c], p_recv.at[c], c).wait_send()
        ctx_copy(hid.at[my_c], hid.at[c], h_send.at[c], h_recv.at[c], c).wait_send()
        group_of(answers, r_send, r_recv, c, lines).wait_send()


def shards(
    n_ctx, n_dp, queries, key_rows, value_rows, stream, norm_gain, expert_ids, gate_values,
    w_gate, w_up, w_down,
):
    tokens, width = stream.shape[1:]
    top = expert_ids.shape[2]
    kv = key_rows.shape[2]
    units = w_gate.shape[2]
    col = width // n_ctx
    slot, chunks = message_form(col)
    rows = n_dp * slot
    lines = rows * chunks
    wide = col // chunks
    order = lines if chunks > 1 else TILE
    bf16, f32 = jnp.bfloat16, jnp.float32
    scratch = [
        ((tokens, queries.shape[2]), bf16),
        ((tokens, width), bf16),
        ((1, width), f32),
        ((top, tokens), jnp.int32),
        ((top, tokens), f32),
        ((col, 2 * units), bf16),
        ((units, col), bf16),
        ((n_ctx, lines, wide), bf16),
        ((n_ctx, lines, wide), bf16),
        ((n_ctx, tokens, kv), bf16),
        ((n_ctx, tokens, kv), bf16),
        ((n_ctx, rows, 2 * units), bf16),
        ((n_ctx, rows, 2 * units), bf16),
        ((rows, 2 * units), f32),
        ((n_ctx, rows, units), bf16),
        ((n_ctx, lines, wide), bf16),
        ((n_ctx, lines, wide), bf16),
        ((chunks * tokens, lines), bf16),
        ((chunks * tokens, lines), bf16),
        ((order, order), bf16),
        ((order, order), bf16),
    ]
    need = sum(math.prod(s) * jnp.dtype(t).itemsize for s, t in scratch)
    hbm = pl.BlockSpec(memory_space=pltpu.HBM)
    vmem = pl.BlockSpec(memory_space=pltpu.VMEM)
    return pl.pallas_call(
        functools.partial(fused, n_ctx, n_dp, 6),
        out_shape=(
            jax.ShapeDtypeStruct(queries.shape, bf16),
            jax.ShapeDtypeStruct(stream.shape, bf16),
        ),
        in_specs=[hbm] * 10,
        out_specs=(vmem, vmem),
        scratch_shapes=[pltpu.VMEM(s, t) for s, t in scratch]
        + [pltpu.SemaphoreType.DMA((n_ctx,))] * 12
        + [pltpu.SemaphoreType.DMA((10,))],
        compiler_params=pltpu.CompilerParams(
            collective_id=0, has_side_effects=True, vmem_limit_bytes=need + (16 << 20)
        ),
    )(
        queries, key_rows, value_rows, stream, norm_gain.reshape(1, width),
        expert_ids.swapaxes(1, 2), gate_values.swapaxes(1, 2), w_gate, w_up, w_down,
    )


def solution(mesh):
    rows = P("dp", "ctx", None)
    return jax.shard_map(
        functools.partial(shards, mesh.shape["ctx"], mesh.shape["dp"]),
        mesh=mesh,
        in_specs=(rows,) * 4 + (P(),) + (rows,) * 4 + (P("dp", None, "ctx"),),
        out_specs=(rows, rows),
        check_vma=False,
    )
```

```python
import functools
import math

import jax
import jax.numpy as jnp
from jax import lax
from jax.experimental import pallas as pl
from jax.experimental.pallas import tpu as pltpu
from jax.sharding import PartitionSpec as P

HD = 128
CAP = 12
TILE = 16
LANES = 128
MESH = pl.DeviceIdType.MESH
hidden_score = -1e30


def message_form(col):
    chunks = col // LANES
    if chunks * CAP % TILE == 0:
        return CAP, chunks
    return TILE, 1


def fused(
    n_ctx, n_dp, split,
    q_hbm, k_hbm, v_hbm, s_hbm, gain_hbm, ids_hbm, gv_hbm, wg_hbm, wu_hbm, wd_hbm,
    att_ref, out_ref,
    q_ref, s_ref, normed_ref, gain_ref, ids_ref, gv_ref, wgu, wd_ref,
    outgoing, arrived, kbuf, vbuf, rs_out, rs_in, own, hid, answers, ret,
    w_hi, w_lo, sort, unsort,
    k_send, k_recv, v_send, v_recv, a_send, a_recv, p_send, p_recv, h_send, h_recv,
    r_send, r_recv, load_sem,
):
    my_c = lax.axis_index("ctx")
    my_d = lax.axis_index("dp")
    me = my_c * n_dp + my_d
    total = n_ctx * n_dp
    tokens, width = s_ref.shape
    col = width // n_ctx
    slot, chunks = message_form(col)
    message = slot * chunks
    wide = col // chunks
    rows_all = n_dp * slot
    lines = n_dp * message
    units = wd_ref.shape[0]
    heads = q_ref.shape[1] // HD
    kv_heads = kbuf.shape[2] // HD
    group = heads // kv_heads

    pairs = (
        (ids_hbm.at[0], ids_ref),
        (gv_hbm.at[0], gv_ref),
        (s_hbm.at[0], s_ref),
        (gain_hbm, gain_ref),
        (wg_hbm.at[0], wgu.at[:, pl.ds(0, units)]),
        (wu_hbm.at[0], wgu.at[:, pl.ds(units, units)]),
        (k_hbm.at[0], kbuf.at[my_c]),
        (v_hbm.at[0], vbuf.at[my_c]),
        (q_hbm.at[0], q_ref),
        (wd_hbm.at[0], wd_ref),
    )
    loads = [pltpu.make_async_copy(a, b, load_sem.at[i]) for i, (a, b) in enumerate(pairs)]
    for load in loads:
        load.start()

    barrier = pltpu.get_barrier_semaphore()

    def greet(i, carry):
        peer = lax.rem(me + i, total)
        pl.semaphore_signal(
            barrier, inc=1, device_id=(peer // n_dp, lax.rem(peer, n_dp)), device_id_type=MESH
        )
        return carry

    lax.fori_loop(1, total, greet, 0)

    def parts_of(line):
        rest = lax.rem(line, message)
        return lax.div(line, message), lax.div(rest, slot), lax.rem(rest, slot)

    expert, chunk, place_rank = parts_of(lax.broadcasted_iota(jnp.int32, (lines, 1), 0))
    _, chunk_lane, rank_lane = parts_of(lax.broadcasted_iota(jnp.int32, (1, lines), 1))
    expert_lane = lax.div(lax.broadcasted_iota(jnp.int32, (1, lines), 1), message)
    loads[0].wait()
    loads[1].wait()
    hot = jnp.zeros((lines, tokens), jnp.float32)
    weight = jnp.zeros((lines, tokens), jnp.float32)
    for t in range(ids_ref.shape[0]):
        hit = ids_ref[t : t + 1, :] == expert
        hot = jnp.where(hit, 1.0, hot)
        weight = jnp.where(hit, gv_ref[t : t + 1, :], weight)
    rows_i = lax.broadcasted_iota(jnp.int32, (tokens, tokens), 0)
    cols_i = lax.broadcasted_iota(jnp.int32, (tokens, tokens), 1)
    before = jnp.where(rows_i < cols_i, 1.0, 0.0).astype(jnp.bfloat16)
    rank = jnp.dot(hot.astype(jnp.bfloat16), before, preferred_element_type=jnp.float32)
    place = jnp.where(rank == place_rank.astype(jnp.float32), hot, 0.0)
    select = jnp.concatenate(
        [jnp.where(chunk == j, place, 0.0).astype(jnp.bfloat16) for j in range(chunks)], axis=1
    )

    pl.semaphore_wait(barrier, total - 1)

    def ctx_copy(src, dst, send, recv, c):
        return pltpu.make_async_remote_copy(
            src_ref=src, dst_ref=dst, send_sem=send, recv_sem=recv,
            device_id=(c, my_d), device_id_type=MESH,
        )

    others = [lax.rem(my_c + i, n_ctx) for i in range(1, n_ctx)]
    my_rows = pl.ds(pl.multiple_of(my_d * message, message), message)

    def scatter(src, dst, send, recv, c, first):
        def one(i, carry):
            d = lax.rem(my_d + i, n_dp)
            pltpu.make_async_remote_copy(
                src_ref=src.at[c, pl.ds(pl.multiple_of(d * message, message), message)],
                dst_ref=dst.at[my_c, my_rows],
                send_sem=send.at[c],
                recv_sem=recv.at[my_c],
                device_id=(c, d),
                device_id_type=MESH,
            ).start()
            return carry

        lax.fori_loop(first, n_dp, one, 0)

    def group_of(buf, send, recv, c, rows):
        part = buf.at[c, pl.ds(0, rows)]
        return pltpu.make_async_remote_copy(
            src_ref=part, dst_ref=part, send_sem=send.at[c], recv_sem=recv.at[c],
            device_id=(c, lax.rem(my_d + 1, n_dp)), device_id_type=MESH,
        )

    for c in others:
        ctx_copy(k_hbm.at[0], kbuf.at[my_c], k_send.at[c], k_recv.at[my_c], c).start()
        ctx_copy(v_hbm.at[0], vbuf.at[my_c], v_send.at[c], v_recv.at[my_c], c).start()

    loads[2].wait()
    loads[3].wait()
    x = s_ref[...].astype(jnp.float32)
    normed = (
        x * lax.rsqrt(jnp.mean(x * x, axis=-1, keepdims=True) + 1e-06) * gain_ref[...]
    ).astype(jnp.bfloat16)
    normed_ref[...] = normed
    for i, c in enumerate(others + [my_c]):
        stacked = jnp.concatenate(
            [
                normed_ref[:, pl.ds(pl.multiple_of(c * col + j * wide, wide), wide)]
                for j in range(chunks)
            ],
            axis=0,
        )
        outgoing[c] = jnp.dot(select, stacked, preferred_element_type=jnp.float32).astype(
            jnp.bfloat16
        )
        scatter(outgoing, arrived, a_send, a_recv, c, 1 if i == n_ctx - 1 else 0)
    arrived[my_c, my_rows] = outgoing[my_c, my_rows]

    if chunks > 1:
        goes = chunk * rows_all + expert * slot + place_rank
        goes_lane = chunk_lane * rows_all + expert_lane * slot + rank_lane
        square = (lines, lines)
        unsort[...] = jnp.where(
            lax.broadcasted_iota(jnp.int32, square, 1) == goes, 1.0, 0.0
        ).astype(jnp.bfloat16)
        sort[...] = jnp.where(
            lax.broadcasted_iota(jnp.int32, square, 0) == goes_lane, 1.0, 0.0
        ).astype(jnp.bfloat16)

    back = (place * weight).T
    for j in range(chunks):
        of_chunk = jnp.where(chunk_lane == j, back, 0.0)
        upper = of_chunk.astype(jnp.bfloat16)
        w_hi[j * tokens : (j + 1) * tokens] = upper
        w_lo[j * tokens : (j + 1) * tokens] = (of_chunk - upper.astype(jnp.float32)).astype(
            jnp.bfloat16
        )

    keys = n_ctx * tokens
    scale = 1.0 / math.sqrt(HD)

    def attend(first, last):
        def one(pair, carry):
            kv_at = pl.ds(pl.multiple_of((2 * pair // group) * HD, HD), HD)
            k_all = kbuf[:, :, kv_at].reshape(keys, HD)
            v_all = vbuf[:, :, kv_at].reshape(keys, HD)
            at = [pl.ds(pl.multiple_of((2 * pair + i) * HD, HD), HD) for i in range(2)]
            two = jnp.concatenate([q_ref[:, a] for a in at], axis=0)
            scores = lax.dot_general(
                two, k_all, (((1,), (1,)), ((), ())), preferred_element_type=jnp.float32
            ) * scale
            q_pos = lax.broadcasted_iota(jnp.int32, (2 * tokens, keys), 0)
            q_pos = my_c * tokens + jnp.where(q_pos < tokens, q_pos, q_pos - tokens)
            k_pos = lax.broadcasted_iota(jnp.int32, (2 * tokens, keys), 1)
            scores = jnp.where(k_pos <= q_pos, scores, hidden_score)
            probs = jnp.exp(scores - jnp.max(scores, axis=-1, keepdims=True))
            mass = jnp.sum(probs, axis=-1, keepdims=True)
            mixed = jnp.dot(probs.astype(jnp.bfloat16), v_all, preferred_element_type=jnp.float32)
            done = (mixed / mass).astype(jnp.bfloat16)
            for i in range(2):
                att_ref[0, :, at[i]] = done[i * tokens : (i + 1) * tokens]
            return carry

        lax.fori_loop(first // 2, last // 2, one, 0)

    marks = [heads * part // 16 for part in split]

    def partial(c):
        block = arrived[c]
        if chunks > 1:
            block = jnp.dot(sort[...], block, preferred_element_type=jnp.float32).astype(
                jnp.bfloat16
            )
            block = jnp.concatenate(
                [block[j * rows_all : (j + 1) * rows_all] for j in range(chunks)], axis=1
            )
        return jnp.dot(block, wgu[...], preferred_element_type=jnp.float32)

    loads[4].wait()
    loads[5].wait()
    for c in others:
        group_of(arrived, a_send, a_recv, c, lines).wait_recv()
        rs_out[c] = partial(c).astype(jnp.bfloat16)
        ctx_copy(rs_out.at[c], rs_in.at[my_c], p_send.at[c], p_recv.at[my_c], c).start()
    group_of(arrived, a_send, a_recv, my_c, lines - message).wait_recv()
    own[...] = partial(my_c)
    for load in loads[6:]:
        load.wait()
    for c in others:
        ctx_copy(k_hbm.at[0], kbuf.at[c], k_send.at[c], k_recv.at[c], c).wait_recv()
        ctx_copy(v_hbm.at[0], vbuf.at[c], v_send.at[c], v_recv.at[c], c).wait_recv()
    attend(0, marks[0])
    for c in others:
        ctx_copy(rs_out.at[c], rs_in.at[c], p_send.at[c], p_recv.at[c], c).wait_recv()
    sums = own[...]
    for c in others:
        sums = sums + rs_in[c].astype(jnp.float32)
    gate = sums[:, :units]
    hid[my_c] = (gate / (1.0 + jnp.exp(-gate)) * sums[:, units:]).astype(jnp.bfloat16)
    for c in others:
        ctx_copy(hid.at[my_c], hid.at[my_c], h_send.at[c], h_recv.at[my_c], c).start()

    def answer(c):
        block = jnp.dot(hid[c], wd_ref[...], preferred_element_type=jnp.float32).astype(
            jnp.bfloat16
        )
        if chunks > 1:
            block = jnp.concatenate(
                [block[:, j * wide : (j + 1) * wide] for j in range(chunks)], axis=0
            )
            block = jnp.dot(unsort[...], block, preferred_element_type=jnp.float32).astype(
                jnp.bfloat16
            )
        answers[c] = block

    answer(my_c)
    scatter(answers, ret, r_send, r_recv, my_c, 1)
    ret[my_c, my_rows] = answers[my_c, my_rows]
    attend(marks[0], marks[1])
    for c in others:
        ctx_copy(hid.at[my_c], hid.at[c], h_send.at[c], h_recv.at[c], c).wait_recv()
        answer(c)
        scatter(answers, ret, r_send, r_recv, c, 0)
    attend(marks[1], heads)

    def combine(c):
        part = ret[c]
        mixed = jnp.dot(w_hi[...], part, preferred_element_type=jnp.float32) + jnp.dot(
            w_lo[...], part, preferred_element_type=jnp.float32
        )
        mixed = jnp.concatenate(
            [mixed[j * tokens : (j + 1) * tokens] for j in range(chunks)], axis=1
        )
        out_ref[0, :, pl.ds(pl.multiple_of(c * col, col), col)] = mixed.astype(jnp.bfloat16)

    group_of(ret, r_send, r_recv, my_c, lines - message).wait_recv()
    combine(my_c)
    for c in others:
        group_of(ret, r_send, r_recv, c, lines).wait_recv()
        combine(c)

    group_of(outgoing, a_send, a_recv, my_c, lines - message).wait_send()
    group_of(answers, r_send, r_recv, my_c, lines - message).wait_send()
    for c in others:
        ctx_copy(k_hbm.at[0], kbuf.at[c], k_send.at[c], k_recv.at[c], c).wait_send()
        ctx_copy(v_hbm.at[0], vbuf.at[c], v_send.at[c], v_recv.at[c], c).wait_send()
        group_of(outgoing, a_send, a_recv, c, lines).wait_send()
        ctx_copy(rs_out.at[c], rs_in.at[c], p_send.at[c], p_recv.at[c], c).wait_send()
        ctx_copy(hid.at[my_c], hid.at[c], h_send.at[c], h_recv.at[c], c).wait_send()
        group_of(answers, r_send, r_recv, c, lines).wait_send()


def shards(
    n_ctx, n_dp, queries, key_rows, value_rows, stream, norm_gain, expert_ids, gate_values,
    w_gate, w_up, w_down,
):
    tokens, width = stream.shape[1:]
    top = expert_ids.shape[2]
    kv = key_rows.shape[2]
    units = w_gate.shape[2]
    col = width // n_ctx
    slot, chunks = message_form(col)
    rows = n_dp * slot
    lines = rows * chunks
    wide = col // chunks
    order = lines if chunks > 1 else TILE
    bf16, f32 = jnp.bfloat16, jnp.float32
    scratch = [
        ((tokens, queries.shape[2]), bf16),
        ((tokens, width), bf16),
        ((tokens, width), bf16),
        ((1, width), f32),
        ((top, tokens), jnp.int32),
        ((top, tokens), f32),
        ((col, 2 * units), bf16),
        ((units, col), bf16),
        ((n_ctx, lines, wide), bf16),
        ((n_ctx, lines, wide), bf16),
        ((n_ctx, tokens, kv), bf16),
        ((n_ctx, tokens, kv), bf16),
        ((n_ctx, rows, 2 * units), bf16),
        ((n_ctx, rows, 2 * units), bf16),
        ((rows, 2 * units), f32),
        ((n_ctx, rows, units), bf16),
        ((n_ctx, lines, wide), bf16),
        ((n_ctx, lines, wide), bf16),
        ((chunks * tokens, lines), bf16),
        ((chunks * tokens, lines), bf16),
        ((order, order), bf16),
        ((order, order), bf16),
    ]
    need = sum(math.prod(s) * jnp.dtype(t).itemsize for s, t in scratch)
    hbm = pl.BlockSpec(memory_space=pltpu.HBM)
    vmem = pl.BlockSpec(memory_space=pltpu.VMEM)
    operands = (
        queries, key_rows, value_rows, stream, norm_gain.reshape(1, width),
        expert_ids.swapaxes(1, 2), gate_values.swapaxes(1, 2), w_gate, w_up, w_down,
    )
    return pl.pallas_call(
        functools.partial(fused, n_ctx, n_dp, (4, 8)),
        out_shape=(
            jax.ShapeDtypeStruct(queries.shape, bf16),
            jax.ShapeDtypeStruct(stream.shape, bf16),
        ),
        in_specs=[hbm] * 10,
        out_specs=(vmem, vmem),
        scratch_shapes=[pltpu.VMEM(s, t) for s, t in scratch]
        + [pltpu.SemaphoreType.DMA((n_ctx,))] * 12
        + [pltpu.SemaphoreType.DMA((10,))],
        compiler_params=pltpu.CompilerParams(
            collective_id=0, has_side_effects=True, vmem_limit_bytes=need + (16 << 20)
        ),
    )(*(pltpu.with_memory_space_constraint(x, pltpu.HBM) for x in operands))


def solution(mesh):
    rows = P("dp", "ctx", None)
    return jax.shard_map(
        functools.partial(shards, mesh.shape["ctx"], mesh.shape["dp"]),
        mesh=mesh,
        in_specs=(rows,) * 4 + (P(),) + (rows,) * 4 + (P("dp", None, "ctx"),),
        out_specs=(rows, rows),
        check_vma=False,
    )
```

```python
import functools
import math

import jax
import jax.numpy as jnp
from jax import lax
from jax.experimental import pallas as pl
from jax.experimental.pallas import tpu as pltpu
from jax.sharding import PartitionSpec as P

HD = 128
CAP = 12
TILE = 16
LANES = 128
MESH = pl.DeviceIdType.MESH
hidden_score = -1e30


def message_form(col):
    chunks = col // LANES
    if chunks * CAP % TILE == 0:
        return CAP, chunks
    return TILE, 1


def fused(
    n_ctx, n_dp, split,
    q_hbm, k_hbm, v_hbm, s_hbm, gain_hbm, ids_hbm, gv_hbm, wg_hbm, wu_hbm, wd_hbm,
    att_ref, out_ref,
    q_ref, s_ref, normed_ref, gain_ref, ids_ref, gv_ref, wgu, wd_ref,
    outgoing, arrived, kbuf, vbuf, rs_out, rs_in, own, hid, answers, ret,
    w_back, probs_ref, mass_ref, sort, unsort,
    k_send, k_recv, v_send, v_recv, a_send, a_recv, p_send, p_recv, h_send, h_recv,
    r_send, r_recv, load_sem,
):
    my_c = lax.axis_index("ctx")
    my_d = lax.axis_index("dp")
    me = my_c * n_dp + my_d
    total = n_ctx * n_dp
    tokens, width = s_ref.shape
    col = width // n_ctx
    slot, chunks = message_form(col)
    message = slot * chunks
    wide = col // chunks
    rows_all = n_dp * slot
    lines = n_dp * message
    units = wd_ref.shape[0]
    heads = q_ref.shape[1] // HD
    kv_heads = kbuf.shape[2] // HD
    group = heads // kv_heads

    pairs = (
        (ids_hbm.at[0], ids_ref),
        (gv_hbm.at[0], gv_ref),
        (s_hbm.at[0], s_ref),
        (gain_hbm, gain_ref),
        (wg_hbm.at[0], wgu.at[:, pl.ds(0, units)]),
        (wu_hbm.at[0], wgu.at[:, pl.ds(units, units)]),
        (k_hbm.at[0], kbuf.at[my_c]),
        (v_hbm.at[0], vbuf.at[my_c]),
        (q_hbm.at[0], q_ref),
        (wd_hbm.at[0], wd_ref),
    )
    loads = [pltpu.make_async_copy(a, b, load_sem.at[i]) for i, (a, b) in enumerate(pairs)]
    for load in loads:
        load.start()

    barrier = pltpu.get_barrier_semaphore()

    def greet(i, carry):
        peer = lax.rem(me + i, total)
        pl.semaphore_signal(
            barrier, inc=1, device_id=(peer // n_dp, lax.rem(peer, n_dp)), device_id_type=MESH
        )
        return carry

    lax.fori_loop(1, total, greet, 0)

    def parts_of(line):
        rest = lax.rem(line, message)
        return lax.div(line, message), lax.div(rest, slot), lax.rem(rest, slot)

    expert, chunk, place_rank = parts_of(lax.broadcasted_iota(jnp.int32, (lines, 1), 0))
    _, chunk_lane, rank_lane = parts_of(lax.broadcasted_iota(jnp.int32, (1, lines), 1))
    expert_lane = lax.div(lax.broadcasted_iota(jnp.int32, (1, lines), 1), message)
    loads[0].wait()
    loads[1].wait()
    hot = jnp.zeros((lines, tokens), jnp.float32)
    weight = jnp.zeros((lines, tokens), jnp.float32)
    for t in range(ids_ref.shape[0]):
        hit = ids_ref[t : t + 1, :] == expert
        hot = jnp.where(hit, 1.0, hot)
        weight = jnp.where(hit, gv_ref[t : t + 1, :], weight)
    rows_i = lax.broadcasted_iota(jnp.int32, (tokens, tokens), 0)
    cols_i = lax.broadcasted_iota(jnp.int32, (tokens, tokens), 1)
    before = jnp.where(rows_i < cols_i, 1.0, 0.0).astype(jnp.bfloat16)
    rank = jnp.dot(hot.astype(jnp.bfloat16), before, preferred_element_type=jnp.float32)
    place = jnp.where(rank == place_rank.astype(jnp.float32), hot, 0.0)
    select = jnp.concatenate(
        [jnp.where(chunk == j, place, 0.0).astype(jnp.bfloat16) for j in range(chunks)], axis=1
    )

    pl.semaphore_wait(barrier, total - 1)

    def ctx_copy(src, dst, send, recv, c):
        return pltpu.make_async_remote_copy(
            src_ref=src, dst_ref=dst, send_sem=send, recv_sem=recv,
            device_id=(c, my_d), device_id_type=MESH,
        )

    others = [lax.rem(my_c + i, n_ctx) for i in range(1, n_ctx)]
    my_rows = pl.ds(pl.multiple_of(my_d * message, message), message)

    def scatter(src, dst, send, recv, c, first):
        def one(i, carry):
            d = lax.rem(my_d + i, n_dp)
            pltpu.make_async_remote_copy(
                src_ref=src.at[c, pl.ds(pl.multiple_of(d * message, message), message)],
                dst_ref=dst.at[my_c, my_rows],
                send_sem=send.at[c],
                recv_sem=recv.at[my_c],
                device_id=(c, d),
                device_id_type=MESH,
            ).start()
            return carry

        lax.fori_loop(first, n_dp, one, 0)

    def group_of(buf, send, recv, c, rows):
        part = buf.at[c, pl.ds(0, rows)]
        return pltpu.make_async_remote_copy(
            src_ref=part, dst_ref=part, send_sem=send.at[c], recv_sem=recv.at[c],
            device_id=(c, lax.rem(my_d + 1, n_dp)), device_id_type=MESH,
        )

    for c in others:
        ctx_copy(k_hbm.at[0], kbuf.at[my_c], k_send.at[c], k_recv.at[my_c], c).start()

    loads[2].wait()
    loads[3].wait()
    x = s_ref[...].astype(jnp.float32)
    normed = (
        x * lax.rsqrt(jnp.mean(x * x, axis=-1, keepdims=True) + 1e-06) * gain_ref[...]
    ).astype(jnp.bfloat16)
    normed_ref[...] = normed
    for i, c in enumerate(others + [my_c]):
        stacked = jnp.concatenate(
            [
                normed_ref[:, pl.ds(pl.multiple_of(c * col + j * wide, wide), wide)]
                for j in range(chunks)
            ],
            axis=0,
        )
        outgoing[c] = jnp.dot(select, stacked, preferred_element_type=jnp.float32).astype(
            jnp.bfloat16
        )
        scatter(outgoing, arrived, a_send, a_recv, c, 1 if i == n_ctx - 1 else 0)
    arrived[my_c, my_rows] = outgoing[my_c, my_rows]

    if chunks > 1:
        goes = chunk * rows_all + expert * slot + place_rank
        goes_lane = chunk_lane * rows_all + expert_lane * slot + rank_lane
        square = (lines, lines)
        unsort[...] = jnp.where(
            lax.broadcasted_iota(jnp.int32, square, 1) == goes, 1.0, 0.0
        ).astype(jnp.bfloat16)
        sort[...] = jnp.where(
            lax.broadcasted_iota(jnp.int32, square, 0) == goes_lane, 1.0, 0.0
        ).astype(jnp.bfloat16)

    back = (place * weight).T
    for j in range(chunks):
        w_back[j * tokens : (j + 1) * tokens] = jnp.where(chunk_lane == j, back, 0.0).astype(
            jnp.bfloat16
        )

    keys = n_ctx * tokens
    scale = 1.0 / math.sqrt(HD)

    def kv_lanes(pair):
        return pl.ds(pl.multiple_of((2 * pair // group) * HD, HD), HD)

    def head_lanes(head):
        return pl.ds(pl.multiple_of(head * HD, HD), HD)

    def weigh(first, last):
        def one(pair, carry):
            two = jnp.concatenate([q_ref[:, head_lanes(2 * pair + i)] for i in range(2)], axis=0)
            scores = lax.dot_general(
                two, kbuf[:, :, kv_lanes(pair)].reshape(keys, HD), (((1,), (1,)), ((), ())),
                preferred_element_type=jnp.float32,
            ) * scale
            q_pos = lax.broadcasted_iota(jnp.int32, (2 * tokens, keys), 0)
            q_pos = my_c * tokens + jnp.where(q_pos < tokens, q_pos, q_pos - tokens)
            k_pos = lax.broadcasted_iota(jnp.int32, (2 * tokens, keys), 1)
            scores = jnp.where(k_pos <= q_pos, scores, hidden_score)
            probs = jnp.exp(scores - jnp.max(scores, axis=-1, keepdims=True))
            mass = jnp.sum(probs, axis=-1, keepdims=True)
            probs_ref[pair] = probs.astype(jnp.bfloat16)
            mass_ref[pair] = jnp.broadcast_to(mass, (2 * tokens, HD))
            return carry

        lax.fori_loop(first, last, one, 0)

    def mix_values():
        def one(pair, carry):
            mixed = jnp.dot(
                probs_ref[pair], vbuf[:, :, kv_lanes(pair)].reshape(keys, HD),
                preferred_element_type=jnp.float32,
            )
            done = (mixed / mass_ref[pair]).astype(jnp.bfloat16)
            for i in range(2):
                att_ref[0, :, head_lanes(2 * pair + i)] = done[i * tokens : (i + 1) * tokens]
            return carry

        lax.fori_loop(0, heads // 2, one, 0)

    marks = [heads // 2 * part // 8 for part in split]
    loads[6].wait()
    loads[8].wait()
    for c in others:
        ctx_copy(k_hbm.at[0], kbuf.at[c], k_send.at[c], k_recv.at[c], c).wait_recv()
    weigh(0, marks[0])

    def partial(c):
        block = arrived[c]
        if chunks > 1:
            block = jnp.dot(sort[...], block, preferred_element_type=jnp.float32).astype(
                jnp.bfloat16
            )
            block = jnp.concatenate(
                [block[j * rows_all : (j + 1) * rows_all] for j in range(chunks)], axis=1
            )
        return jnp.dot(block, wgu[...], preferred_element_type=jnp.float32)

    loads[4].wait()
    loads[5].wait()
    for c in others:
        group_of(arrived, a_send, a_recv, c, lines).wait_recv()
        rs_out[c] = partial(c).astype(jnp.bfloat16)
        ctx_copy(rs_out.at[c], rs_in.at[my_c], p_send.at[c], p_recv.at[my_c], c).start()
    group_of(arrived, a_send, a_recv, my_c, lines - message).wait_recv()
    own[...] = partial(my_c)
    loads[7].wait()
    loads[9].wait()
    weigh(marks[0], marks[1])
    for c in others:
        ctx_copy(rs_out.at[c], rs_in.at[c], p_send.at[c], p_recv.at[c], c).wait_recv()
    sums = own[...]
    for c in others:
        sums = sums + rs_in[c].astype(jnp.float32)
    gate = sums[:, :units]
    hid[my_c] = (gate / (1.0 + jnp.exp(-gate)) * sums[:, units:]).astype(jnp.bfloat16)
    for c in others:
        ctx_copy(hid.at[my_c], hid.at[my_c], h_send.at[c], h_recv.at[my_c], c).start()
    for c in others:
        ctx_copy(v_hbm.at[0], vbuf.at[my_c], v_send.at[c], v_recv.at[my_c], c).start()

    def answer(c):
        block = jnp.dot(hid[c], wd_ref[...], preferred_element_type=jnp.float32).astype(
            jnp.bfloat16
        )
        if chunks > 1:
            block = jnp.concatenate(
                [block[:, j * wide : (j + 1) * wide] for j in range(chunks)], axis=0
            )
            block = jnp.dot(unsort[...], block, preferred_element_type=jnp.float32).astype(
                jnp.bfloat16
            )
        answers[c] = block

    answer(my_c)
    scatter(answers, ret, r_send, r_recv, my_c, 1)
    ret[my_c, my_rows] = answers[my_c, my_rows]
    weigh(marks[1], heads // 2)
    for c in others:
        ctx_copy(hid.at[my_c], hid.at[c], h_send.at[c], h_recv.at[c], c).wait_recv()
        answer(c)
        scatter(answers, ret, r_send, r_recv, c, 0)
    for c in others:
        ctx_copy(v_hbm.at[0], vbuf.at[c], v_send.at[c], v_recv.at[c], c).wait_recv()
    mix_values()

    def combine(c):
        part = ret[c]
        mixed = jnp.dot(w_back[...], part, preferred_element_type=jnp.float32)
        mixed = jnp.concatenate(
            [mixed[j * tokens : (j + 1) * tokens] for j in range(chunks)], axis=1
        )
        out_ref[0, :, pl.ds(pl.multiple_of(c * col, col), col)] = mixed.astype(jnp.bfloat16)

    group_of(ret, r_send, r_recv, my_c, lines - message).wait_recv()
    combine(my_c)
    for c in others:
        group_of(ret, r_send, r_recv, c, lines).wait_recv()
        combine(c)

    group_of(outgoing, a_send, a_recv, my_c, lines - message).wait_send()
    group_of(answers, r_send, r_recv, my_c, lines - message).wait_send()
    for c in others:
        ctx_copy(k_hbm.at[0], kbuf.at[c], k_send.at[c], k_recv.at[c], c).wait_send()
        ctx_copy(v_hbm.at[0], vbuf.at[c], v_send.at[c], v_recv.at[c], c).wait_send()
        group_of(outgoing, a_send, a_recv, c, lines).wait_send()
        ctx_copy(rs_out.at[c], rs_in.at[c], p_send.at[c], p_recv.at[c], c).wait_send()
        ctx_copy(hid.at[my_c], hid.at[c], h_send.at[c], h_recv.at[c], c).wait_send()
        group_of(answers, r_send, r_recv, c, lines).wait_send()


def shards(
    n_ctx, n_dp, queries, key_rows, value_rows, stream, norm_gain, expert_ids, gate_values,
    w_gate, w_up, w_down,
):
    tokens, width = stream.shape[1:]
    top = expert_ids.shape[2]
    kv = key_rows.shape[2]
    units = w_gate.shape[2]
    col = width // n_ctx
    slot, chunks = message_form(col)
    rows = n_dp * slot
    lines = rows * chunks
    wide = col // chunks
    heads = queries.shape[2] // HD
    order = lines if chunks > 1 else TILE
    bf16, f32 = jnp.bfloat16, jnp.float32
    scratch = [
        ((tokens, queries.shape[2]), bf16),
        ((tokens, width), bf16),
        ((tokens, width), bf16),
        ((1, width), f32),
        ((top, tokens), jnp.int32),
        ((top, tokens), f32),
        ((col, 2 * units), bf16),
        ((units, col), bf16),
        ((n_ctx, lines, wide), bf16),
        ((n_ctx, lines, wide), bf16),
        ((n_ctx, tokens, kv), bf16),
        ((n_ctx, tokens, kv), bf16),
        ((n_ctx, rows, 2 * units), bf16),
        ((n_ctx, rows, 2 * units), bf16),
        ((rows, 2 * units), f32),
        ((n_ctx, rows, units), bf16),
        ((n_ctx, lines, wide), bf16),
        ((n_ctx, lines, wide), bf16),
        ((chunks * tokens, lines), bf16),
        ((heads // 2, 2 * tokens, n_ctx * tokens), bf16),
        ((heads // 2, 2 * tokens, HD), f32),
        ((order, order), bf16),
        ((order, order), bf16),
    ]
    need = sum(math.prod(s) * jnp.dtype(t).itemsize for s, t in scratch)
    hbm = pl.BlockSpec(memory_space=pltpu.HBM)
    vmem = pl.BlockSpec(memory_space=pltpu.VMEM)
    operands = (
        queries, key_rows, value_rows, stream, norm_gain.reshape(1, width),
        expert_ids.swapaxes(1, 2), gate_values.swapaxes(1, 2), w_gate, w_up, w_down,
    )
    return pl.pallas_call(
        functools.partial(fused, n_ctx, n_dp, (4, 6)),
        out_shape=(
            jax.ShapeDtypeStruct(queries.shape, bf16),
            jax.ShapeDtypeStruct(stream.shape, bf16),
        ),
        in_specs=[hbm] * 10,
        out_specs=(vmem, vmem),
        scratch_shapes=[pltpu.VMEM(s, t) for s, t in scratch]
        + [pltpu.SemaphoreType.DMA((n_ctx,))] * 12
        + [pltpu.SemaphoreType.DMA((10,))],
        compiler_params=pltpu.CompilerParams(
            collective_id=0, has_side_effects=True, vmem_limit_bytes=need + (16 << 20)
        ),
    )(*(pltpu.with_memory_space_constraint(x, pltpu.HBM) for x in operands))


def solution(mesh):
    rows = P("dp", "ctx", None)
    return jax.shard_map(
        functools.partial(shards, mesh.shape["ctx"], mesh.shape["dp"]),
        mesh=mesh,
        in_specs=(rows,) * 4 + (P(),) + (rows,) * 4 + (P("dp", None, "ctx"),),
        out_specs=(rows, rows),
        check_vma=False,
    )
```

```python
import functools
import math

import jax
import jax.numpy as jnp
from jax import lax
from jax.experimental import pallas as pl
from jax.experimental.pallas import tpu as pltpu
from jax.sharding import PartitionSpec as P

HD = 128
CAP = 12
TILE = 16
LANES = 128
MESH = pl.DeviceIdType.MESH
hidden_score = -1e30


def message_form(col):
    chunks = col // LANES
    if chunks * CAP % TILE == 0:
        return CAP, chunks
    return TILE, 1


def fused(
    n_ctx, n_dp, split,
    q_hbm, k_hbm, v_hbm, s_hbm, gain_hbm, ids_hbm, gv_hbm, wg_hbm, wu_hbm, wd_hbm,
    att_ref, out_ref,
    q_ref, s_ref, normed_ref, gain_ref, ids_ref, gv_ref, wgu, wd_ref,
    outgoing, arrived, kbuf, vbuf, rs_out, rs_in, own, hid, answers, ret,
    w_back, bias_ref, probs_ref, mass_ref, sort, unsort,
    k_send, k_recv, v_send, v_recv, a_send, a_recv, p_send, p_recv, h_send, h_recv,
    r_send, r_recv, load_sem,
):
    my_c = lax.axis_index("ctx")
    my_d = lax.axis_index("dp")
    me = my_c * n_dp + my_d
    total = n_ctx * n_dp
    tokens, width = s_ref.shape
    col = width // n_ctx
    slot, chunks = message_form(col)
    message = slot * chunks
    wide = col // chunks
    rows_all = n_dp * slot
    lines = n_dp * message
    units = wd_ref.shape[0]
    heads = q_ref.shape[1] // HD
    kv_heads = kbuf.shape[2] // HD
    group = heads // kv_heads

    pairs = (
        (ids_hbm.at[0], ids_ref),
        (gv_hbm.at[0], gv_ref),
        (s_hbm.at[0], s_ref),
        (gain_hbm, gain_ref),
        (wg_hbm.at[0], wgu.at[:, pl.ds(0, units)]),
        (wu_hbm.at[0], wgu.at[:, pl.ds(units, units)]),
        (k_hbm.at[0], kbuf.at[my_c]),
        (v_hbm.at[0], vbuf.at[my_c]),
        (q_hbm.at[0], q_ref),
        (wd_hbm.at[0], wd_ref),
    )
    loads = [pltpu.make_async_copy(a, b, load_sem.at[i]) for i, (a, b) in enumerate(pairs)]
    for load in loads:
        load.start()

    barrier = pltpu.get_barrier_semaphore()

    def greet(i, carry):
        peer = lax.rem(me + i, total)
        pl.semaphore_signal(
            barrier, inc=1, device_id=(peer // n_dp, lax.rem(peer, n_dp)), device_id_type=MESH
        )
        return carry

    lax.fori_loop(1, total, greet, 0)

    def whole_part(number, size):
        return jnp.floor((number + 0.5) * (1.0 / size))

    def parts_of(shape, dim):
        line = lax.broadcasted_iota(jnp.int32, shape, dim).astype(jnp.float32)
        owner = whole_part(line, message)
        rest = line - owner * message
        piece = whole_part(rest, slot)
        return owner, piece, rest - piece * slot

    expert, chunk, place_rank = parts_of((lines, 1), 0)
    expert_lane, chunk_lane, rank_lane = parts_of((1, lines), 1)
    expert_id = expert.astype(jnp.int32)
    loads[0].wait()
    loads[1].wait()
    hot = jnp.zeros((lines, tokens), jnp.float32)
    weight = jnp.zeros((lines, tokens), jnp.float32)
    for t in range(ids_ref.shape[0]):
        hit = ids_ref[t : t + 1, :] == expert_id
        hot = jnp.where(hit, 1.0, hot)
        weight = jnp.where(hit, gv_ref[t : t + 1, :], weight)
    rows_i = lax.broadcasted_iota(jnp.int32, (tokens, tokens), 0)
    cols_i = lax.broadcasted_iota(jnp.int32, (tokens, tokens), 1)
    before = jnp.where(rows_i < cols_i, 1.0, 0.0).astype(jnp.bfloat16)
    rank = jnp.dot(hot.astype(jnp.bfloat16), before, preferred_element_type=jnp.float32)
    place = jnp.where(rank == place_rank, hot, 0.0)
    select = jnp.concatenate(
        [jnp.where(chunk == j, place, 0.0).astype(jnp.bfloat16) for j in range(chunks)], axis=1
    )

    pl.semaphore_wait(barrier, total - 1)

    def ctx_copy(src, dst, send, recv, c):
        return pltpu.make_async_remote_copy(
            src_ref=src, dst_ref=dst, send_sem=send, recv_sem=recv,
            device_id=(c, my_d), device_id_type=MESH,
        )

    others = [lax.rem(my_c + i, n_ctx) for i in range(1, n_ctx)]
    my_rows = pl.ds(pl.multiple_of(my_d * message, message), message)

    def scatter(src, dst, send, recv, c, first):
        def one(i, carry):
            d = lax.rem(my_d + i, n_dp)
            pltpu.make_async_remote_copy(
                src_ref=src.at[c, pl.ds(pl.multiple_of(d * message, message), message)],
                dst_ref=dst.at[my_c, my_rows],
                send_sem=send.at[c],
                recv_sem=recv.at[my_c],
                device_id=(c, d),
                device_id_type=MESH,
            ).start()
            return carry

        lax.fori_loop(first, n_dp, one, 0, unroll=n_dp <= 8)

    def group_of(buf, send, recv, c, rows):
        part = buf.at[c, pl.ds(0, rows)]
        return pltpu.make_async_remote_copy(
            src_ref=part, dst_ref=part, send_sem=send.at[c], recv_sem=recv.at[c],
            device_id=(c, lax.rem(my_d + 1, n_dp)), device_id_type=MESH,
        )

    for c in others:
        ctx_copy(k_hbm.at[0], kbuf.at[my_c], k_send.at[c], k_recv.at[my_c], c).start()

    loads[2].wait()
    loads[3].wait()
    x = s_ref[...].astype(jnp.float32)
    normed = (
        x * lax.rsqrt(jnp.mean(x * x, axis=-1, keepdims=True) + 1e-06) * gain_ref[...]
    ).astype(jnp.bfloat16)
    normed_ref[...] = normed
    for i, c in enumerate(others + [my_c]):
        stacked = jnp.concatenate(
            [
                normed_ref[:, pl.ds(pl.multiple_of(c * col + j * wide, wide), wide)]
                for j in range(chunks)
            ],
            axis=0,
        )
        outgoing[c] = jnp.dot(select, stacked, preferred_element_type=jnp.float32).astype(
            jnp.bfloat16
        )
        scatter(outgoing, arrived, a_send, a_recv, c, 1 if i == n_ctx - 1 else 0)
    arrived[my_c, my_rows] = outgoing[my_c, my_rows]

    if chunks > 1:
        goes = (chunk * rows_all + expert * slot + place_rank).astype(jnp.int32)
        goes_lane = (chunk_lane * rows_all + expert_lane * slot + rank_lane).astype(jnp.int32)
        square = (lines, lines)
        unsort[...] = jnp.where(
            lax.broadcasted_iota(jnp.int32, square, 1) == goes, 1.0, 0.0
        ).astype(jnp.bfloat16)
        sort[...] = jnp.where(
            lax.broadcasted_iota(jnp.int32, square, 0) == goes_lane, 1.0, 0.0
        ).astype(jnp.bfloat16)

    back = (place * weight).T
    for j in range(chunks):
        w_back[j * tokens : (j + 1) * tokens] = jnp.where(chunk_lane == j, back, 0.0).astype(
            jnp.bfloat16
        )

    keys = n_ctx * tokens
    scale = math.log2(math.e) / math.sqrt(HD)
    q_pos = my_c * tokens + lax.broadcasted_iota(jnp.int32, (tokens, keys), 0)
    k_pos = lax.broadcasted_iota(jnp.int32, (tokens, keys), 1)
    bias_ref[...] = jnp.where(k_pos <= q_pos, 0.0, hidden_score)

    def kv_lanes(pair):
        return pl.ds(pl.multiple_of((2 * pair // group) * HD, HD), HD)

    def head_lanes(head):
        return pl.ds(pl.multiple_of(head * HD, HD), HD)

    def weigh(first, last):
        def one(pair, carry):
            two = jnp.concatenate([q_ref[:, head_lanes(2 * pair + i)] for i in range(2)], axis=0)
            scores = lax.dot_general(
                two, kbuf[:, :, kv_lanes(pair)].reshape(keys, HD), (((1,), (1,)), ((), ())),
                preferred_element_type=jnp.float32,
            ) * scale
            bias = bias_ref[...]
            scores = scores + jnp.concatenate([bias, bias], axis=0)
            probs = jnp.exp2(scores - jnp.max(scores, axis=-1, keepdims=True))
            mass = jnp.sum(probs, axis=-1, keepdims=True)
            probs_ref[pair] = probs.astype(jnp.bfloat16)
            mass_ref[pair] = jnp.broadcast_to(mass, (2 * tokens, HD))
            return carry

        lax.fori_loop(first, last, one, 0)

    def mix_pair(pair):
        mixed = jnp.dot(
            probs_ref[pair], vbuf[:, :, kv_lanes(pair)].reshape(keys, HD),
            preferred_element_type=jnp.float32,
        )
        done = (mixed / mass_ref[pair]).astype(jnp.bfloat16)
        for i in range(2):
            att_ref[0, :, head_lanes(2 * pair + i)] = done[i * tokens : (i + 1) * tokens]

    def mix_values():
        def one(step, carry):
            mix_pair(2 * step)
            mix_pair(2 * step + 1)
            return carry

        lax.fori_loop(0, heads // 4, one, 0)

    marks = [heads // 2 * part // 8 for part in split]
    loads[6].wait()
    loads[8].wait()
    for c in others:
        ctx_copy(k_hbm.at[0], kbuf.at[c], k_send.at[c], k_recv.at[c], c).wait_recv()
    weigh(0, marks[0])

    def partial(c):
        block = arrived[c]
        if chunks > 1:
            block = jnp.dot(sort[...], block, preferred_element_type=jnp.float32).astype(
                jnp.bfloat16
            )
            block = jnp.concatenate(
                [block[j * rows_all : (j + 1) * rows_all] for j in range(chunks)], axis=1
            )
        return jnp.dot(block, wgu[...], preferred_element_type=jnp.float32)

    loads[4].wait()
    loads[5].wait()
    for c in others:
        group_of(arrived, a_send, a_recv, c, lines).wait_recv()
        rs_out[c] = partial(c).astype(jnp.bfloat16)
        ctx_copy(rs_out.at[c], rs_in.at[my_c], p_send.at[c], p_recv.at[my_c], c).start()
    group_of(arrived, a_send, a_recv, my_c, lines - message).wait_recv()
    own[...] = partial(my_c)
    loads[7].wait()
    loads[9].wait()
    weigh(marks[0], marks[1])
    for c in others:
        ctx_copy(rs_out.at[c], rs_in.at[c], p_send.at[c], p_recv.at[c], c).wait_recv()
    sums = own[...]
    for c in others:
        sums = sums + rs_in[c].astype(jnp.float32)
    gate = sums[:, :units]
    hid[my_c] = (gate / (1.0 + jnp.exp(-gate)) * sums[:, units:]).astype(jnp.bfloat16)
    for c in others:
        ctx_copy(hid.at[my_c], hid.at[my_c], h_send.at[c], h_recv.at[my_c], c).start()
    for c in others:
        ctx_copy(v_hbm.at[0], vbuf.at[my_c], v_send.at[c], v_recv.at[my_c], c).start()

    def answer(c):
        block = jnp.dot(hid[c], wd_ref[...], preferred_element_type=jnp.float32).astype(
            jnp.bfloat16
        )
        if chunks > 1:
            block = jnp.concatenate(
                [block[:, j * wide : (j + 1) * wide] for j in range(chunks)], axis=0
            )
            block = jnp.dot(unsort[...], block, preferred_element_type=jnp.float32).astype(
                jnp.bfloat16
            )
        answers[c] = block

    answer(my_c)
    scatter(answers, ret, r_send, r_recv, my_c, 1)
    ret[my_c, my_rows] = answers[my_c, my_rows]
    weigh(marks[1], heads // 2)
    for c in others:
        ctx_copy(hid.at[my_c], hid.at[c], h_send.at[c], h_recv.at[c], c).wait_recv()
        answer(c)
        scatter(answers, ret, r_send, r_recv, c, 0)
    for c in others:
        ctx_copy(v_hbm.at[0], vbuf.at[c], v_send.at[c], v_recv.at[c], c).wait_recv()
    mix_values()

    def combine(c):
        part = ret[c]
        mixed = jnp.dot(w_back[...], part, preferred_element_type=jnp.float32)
        mixed = jnp.concatenate(
            [mixed[j * tokens : (j + 1) * tokens] for j in range(chunks)], axis=1
        )
        out_ref[0, :, pl.ds(pl.multiple_of(c * col, col), col)] = mixed.astype(jnp.bfloat16)

    group_of(ret, r_send, r_recv, my_c, lines - message).wait_recv()
    combine(my_c)
    for c in others:
        group_of(ret, r_send, r_recv, c, lines).wait_recv()
        combine(c)

    group_of(outgoing, a_send, a_recv, my_c, lines - message).wait_send()
    group_of(answers, r_send, r_recv, my_c, lines - message).wait_send()
    for c in others:
        ctx_copy(k_hbm.at[0], kbuf.at[c], k_send.at[c], k_recv.at[c], c).wait_send()
        ctx_copy(v_hbm.at[0], vbuf.at[c], v_send.at[c], v_recv.at[c], c).wait_send()
        group_of(outgoing, a_send, a_recv, c, lines).wait_send()
        ctx_copy(rs_out.at[c], rs_in.at[c], p_send.at[c], p_recv.at[c], c).wait_send()
        ctx_copy(hid.at[my_c], hid.at[c], h_send.at[c], h_recv.at[c], c).wait_send()
        group_of(answers, r_send, r_recv, c, lines).wait_send()


def write_out(att_ref, out_ref, att_hbm, out_hbm, sems):
    copies = [
        pltpu.make_async_copy(att_ref, att_hbm, sems.at[0]),
        pltpu.make_async_copy(out_ref, out_hbm, sems.at[1]),
    ]
    for copy in copies:
        copy.start()
    for copy in copies:
        copy.wait()


def shards(
    n_ctx, n_dp, queries, key_rows, value_rows, stream, norm_gain, expert_ids, gate_values,
    w_gate, w_up, w_down,
):
    tokens, width = stream.shape[1:]
    top = expert_ids.shape[2]
    kv = key_rows.shape[2]
    units = w_gate.shape[2]
    col = width // n_ctx
    slot, chunks = message_form(col)
    rows = n_dp * slot
    lines = rows * chunks
    wide = col // chunks
    heads = queries.shape[2] // HD
    order = lines if chunks > 1 else TILE
    bf16, f32 = jnp.bfloat16, jnp.float32
    scratch = [
        ((tokens, queries.shape[2]), bf16),
        ((tokens, width), bf16),
        ((tokens, width), bf16),
        ((1, width), f32),
        ((top, tokens), jnp.int32),
        ((top, tokens), f32),
        ((col, 2 * units), bf16),
        ((units, col), bf16),
        ((n_ctx, lines, wide), bf16),
        ((n_ctx, lines, wide), bf16),
        ((n_ctx, tokens, kv), bf16),
        ((n_ctx, tokens, kv), bf16),
        ((n_ctx, rows, 2 * units), bf16),
        ((n_ctx, rows, 2 * units), bf16),
        ((rows, 2 * units), f32),
        ((n_ctx, rows, units), bf16),
        ((n_ctx, lines, wide), bf16),
        ((n_ctx, lines, wide), bf16),
        ((chunks * tokens, lines), bf16),
        ((tokens, n_ctx * tokens), f32),
        ((heads // 2, 2 * tokens, n_ctx * tokens), bf16),
        ((heads // 2, 2 * tokens, HD), f32),
        ((order, order), bf16),
        ((order, order), bf16),
    ]
    need = sum(math.prod(s) * jnp.dtype(t).itemsize for s, t in scratch)
    hbm = pl.BlockSpec(memory_space=pltpu.HBM)
    vmem = pl.BlockSpec(memory_space=pltpu.VMEM)
    operands = (
        queries, key_rows, value_rows, stream, norm_gain.reshape(1, width),
        expert_ids.swapaxes(1, 2), gate_values.swapaxes(1, 2), w_gate, w_up, w_down,
    )
    results = pl.pallas_call(
        functools.partial(fused, n_ctx, n_dp, (4, 6)),
        out_shape=(
            jax.ShapeDtypeStruct(queries.shape, bf16),
            jax.ShapeDtypeStruct(stream.shape, bf16),
        ),
        in_specs=[hbm] * 10,
        out_specs=(vmem, vmem),
        scratch_shapes=[pltpu.VMEM(s, t) for s, t in scratch]
        + [pltpu.SemaphoreType.DMA((n_ctx,))] * 12
        + [pltpu.SemaphoreType.DMA((10,))],
        compiler_params=pltpu.CompilerParams(
            collective_id=0, has_side_effects=True, vmem_limit_bytes=need + (16 << 20)
        ),
    )(*(pltpu.with_memory_space_constraint(x, pltpu.HBM) for x in operands))
    return pl.pallas_call(
        write_out,
        out_shape=tuple(jax.ShapeDtypeStruct(r.shape, r.dtype) for r in results),
        in_specs=[vmem, vmem],
        out_specs=(hbm, hbm),
        scratch_shapes=[pltpu.SemaphoreType.DMA((2,))],
        compiler_params=pltpu.CompilerParams(vmem_limit_bytes=8 << 20),
    )(*results)


def solution(mesh):
    rows = P("dp", "ctx", None)
    return jax.shard_map(
        functools.partial(shards, mesh.shape["ctx"], mesh.shape["dp"]),
        mesh=mesh,
        in_specs=(rows,) * 4 + (P(),) + (rows,) * 4 + (P("dp", None, "ctx"),),
        out_specs=(rows, rows),
        check_vma=False,
    )
```

```python
import functools
import math

import jax
import jax.numpy as jnp
from jax import lax
from jax.experimental import pallas as pl
from jax.experimental.pallas import tpu as pltpu
from jax.sharding import PartitionSpec as P

HD = 128
CAP = 12
TILE = 16
LANES = 128
MESH = pl.DeviceIdType.MESH
hidden_score = -1e30


def message_form(col):
    chunks = col // LANES
    if chunks * CAP % TILE == 0:
        return CAP, chunks
    return TILE, 1


def fused(
    n_ctx, n_dp, split,
    q_hbm, k_hbm, v_hbm, s_hbm, gain_hbm, ids_hbm, gv_hbm, wg_hbm, wu_hbm, wd_hbm,
    att_ref, out_ref,
    q_ref, s_ref, normed_ref, gain_ref, ids_ref, gv_ref, wgu, wd_ref,
    outgoing, arrived, kbuf, vbuf, rs_out, rs_in, own, hid, answers, ret,
    w_back, bias_ref, probs_ref, mass_ref, sort, unsort,
    k_send, k_recv, v_send, v_recv, a_send, a_recv, p_send, p_recv, h_send, h_recv,
    r_send, r_recv, load_sem,
):
    my_c = lax.axis_index("ctx")
    my_d = lax.axis_index("dp")
    me = my_c * n_dp + my_d
    total = n_ctx * n_dp
    tokens, width = s_ref.shape
    col = width // n_ctx
    slot, chunks = message_form(col)
    message = slot * chunks
    wide = col // chunks
    rows_all = n_dp * slot
    lines = n_dp * message
    units = wd_ref.shape[0]
    heads = q_ref.shape[1] // HD
    kv_heads = kbuf.shape[2] // HD
    group = heads // kv_heads

    pairs = (
        (ids_hbm.at[0], ids_ref),
        (gv_hbm.at[0], gv_ref),
        (s_hbm.at[0], s_ref),
        (gain_hbm, gain_ref),
        (wg_hbm.at[0], wgu.at[:, pl.ds(0, units)]),
        (wu_hbm.at[0], wgu.at[:, pl.ds(units, units)]),
        (k_hbm.at[0], kbuf.at[my_c]),
        (v_hbm.at[0], vbuf.at[my_c]),
        (q_hbm.at[0], q_ref),
        (wd_hbm.at[0], wd_ref),
    )
    loads = [pltpu.make_async_copy(a, b, load_sem.at[i]) for i, (a, b) in enumerate(pairs)]
    for load in loads:
        load.start()

    barrier = pltpu.get_barrier_semaphore()

    def greet(i, carry):
        peer = lax.rem(me + i, total)
        pl.semaphore_signal(
            barrier, inc=1, device_id=(peer // n_dp, lax.rem(peer, n_dp)), device_id_type=MESH
        )
        return carry

    lax.fori_loop(1, total, greet, 0)

    for c in range(1, n_ctx):

        @pl.when(c > my_c)
        def _(c=c):
            kbuf[c] = jnp.zeros_like(kbuf[c])
            vbuf[c] = jnp.zeros_like(vbuf[c])

    def whole_part(number, size):
        return jnp.floor((number + 0.5) * (1.0 / size))

    def parts_of(shape, dim):
        line = lax.broadcasted_iota(jnp.int32, shape, dim).astype(jnp.float32)
        owner = whole_part(line, message)
        rest = line - owner * message
        piece = whole_part(rest, slot)
        return owner, piece, rest - piece * slot

    expert, chunk, place_rank = parts_of((lines, 1), 0)
    expert_lane, chunk_lane, rank_lane = parts_of((1, lines), 1)
    expert_id = expert.astype(jnp.int32)
    loads[0].wait()
    loads[1].wait()
    hot = jnp.zeros((lines, tokens), jnp.float32)
    weight = jnp.zeros((lines, tokens), jnp.float32)
    for t in range(ids_ref.shape[0]):
        hit = ids_ref[t : t + 1, :] == expert_id
        hot = jnp.where(hit, 1.0, hot)
        weight = jnp.where(hit, gv_ref[t : t + 1, :], weight)
    rows_i = lax.broadcasted_iota(jnp.int32, (tokens, tokens), 0)
    cols_i = lax.broadcasted_iota(jnp.int32, (tokens, tokens), 1)
    before = jnp.where(rows_i < cols_i, 1.0, 0.0).astype(jnp.bfloat16)
    rank = jnp.dot(hot.astype(jnp.bfloat16), before, preferred_element_type=jnp.float32)
    place = jnp.where(rank == place_rank, hot, 0.0)
    select = jnp.concatenate(
        [jnp.where(chunk == j, place, 0.0).astype(jnp.bfloat16) for j in range(chunks)], axis=1
    )

    pl.semaphore_wait(barrier, total - 1)

    def ctx_copy(src, dst, send, recv, c):
        return pltpu.make_async_remote_copy(
            src_ref=src, dst_ref=dst, send_sem=send, recv_sem=recv,
            device_id=(c, my_d), device_id_type=MESH,
        )

    others = [lax.rem(my_c + i, n_ctx) for i in range(1, n_ctx)]
    my_rows = pl.ds(pl.multiple_of(my_d * message, message), message)

    half = n_dp // 2
    side = my_d // half

    def nth_peer(i):
        far = jnp.int32(i < half)
        step = lax.rem(my_d + i + 1 - far, half)
        return lax.rem(side + far, 2) * half + step

    def scatter(src, dst, send, recv, c, last):
        def one(i, carry):
            d = nth_peer(i)
            pltpu.make_async_remote_copy(
                src_ref=src.at[c, pl.ds(pl.multiple_of(d * message, message), message)],
                dst_ref=dst.at[my_c, my_rows],
                send_sem=send.at[c],
                recv_sem=recv.at[my_c],
                device_id=(c, d),
                device_id_type=MESH,
            ).start()
            return carry

        lax.fori_loop(0, last, one, 0, unroll=n_dp <= 8)

    def group_of(buf, send, recv, c, rows):
        part = buf.at[c, pl.ds(0, rows)]
        return pltpu.make_async_remote_copy(
            src_ref=part, dst_ref=part, send_sem=send.at[c], recv_sem=recv.at[c],
            device_id=(c, lax.rem(my_d + 1, n_dp)), device_id_type=MESH,
        )

    for c in others:

        @pl.when(c > my_c)
        def _(c=c):
            ctx_copy(k_hbm.at[0], kbuf.at[my_c], k_send.at[c], k_recv.at[my_c], c).start()


    loads[2].wait()
    loads[3].wait()
    x = s_ref[...].astype(jnp.float32)
    normed = (
        x * lax.rsqrt(jnp.mean(x * x, axis=-1, keepdims=True) + 1e-06) * gain_ref[...]
    ).astype(jnp.bfloat16)
    normed_ref[...] = normed
    for i, c in enumerate(others + [my_c]):
        stacked = jnp.concatenate(
            [
                normed_ref[:, pl.ds(pl.multiple_of(c * col + j * wide, wide), wide)]
                for j in range(chunks)
            ],
            axis=0,
        )
        outgoing[c] = jnp.dot(select, stacked, preferred_element_type=jnp.float32).astype(
            jnp.bfloat16
        )
        scatter(outgoing, arrived, a_send, a_recv, c, n_dp - 1 if i == n_ctx - 1 else n_dp)
    arrived[my_c, my_rows] = outgoing[my_c, my_rows]

    if chunks > 1:
        goes = (chunk * rows_all + expert * slot + place_rank).astype(jnp.int32)
        goes_lane = (chunk_lane * rows_all + expert_lane * slot + rank_lane).astype(jnp.int32)
        square = (lines, lines)
        unsort[...] = jnp.where(
            lax.broadcasted_iota(jnp.int32, square, 1) == goes, 1.0, 0.0
        ).astype(jnp.bfloat16)
        sort[...] = jnp.where(
            lax.broadcasted_iota(jnp.int32, square, 0) == goes_lane, 1.0, 0.0
        ).astype(jnp.bfloat16)

    back = (place * weight).T
    for j in range(chunks):
        w_back[j * tokens : (j + 1) * tokens] = jnp.where(chunk_lane == j, back, 0.0).astype(
            jnp.bfloat16
        )

    keys = n_ctx * tokens
    scale = math.log2(math.e) / math.sqrt(HD)
    q_pos = my_c * tokens + lax.broadcasted_iota(jnp.int32, (tokens, keys), 0)
    k_pos = lax.broadcasted_iota(jnp.int32, (tokens, keys), 1)
    bias_ref[...] = jnp.where(k_pos <= q_pos, 0.0, hidden_score)

    def kv_lanes(pair):
        return pl.ds(pl.multiple_of((2 * pair // group) * HD, HD), HD)

    def head_lanes(head):
        return pl.ds(pl.multiple_of(head * HD, HD), HD)

    def weigh(first, last):
        def one(pair, carry):
            two = jnp.concatenate([q_ref[:, head_lanes(2 * pair + i)] for i in range(2)], axis=0)
            scores = lax.dot_general(
                two, kbuf[:, :, kv_lanes(pair)].reshape(keys, HD), (((1,), (1,)), ((), ())),
                preferred_element_type=jnp.float32,
            ) * scale
            bias = bias_ref[...]
            scores = scores + jnp.concatenate([bias, bias], axis=0)
            probs = jnp.exp2(scores - jnp.max(scores, axis=-1, keepdims=True))
            mass = jnp.sum(probs, axis=-1, keepdims=True)
            probs_ref[pair] = probs.astype(jnp.bfloat16)
            mass_ref[pair] = jnp.broadcast_to(mass, (2 * tokens, HD))
            return carry

        lax.fori_loop(first, last, one, 0)

    def mix_pair(pair):
        mixed = jnp.dot(
            probs_ref[pair], vbuf[:, :, kv_lanes(pair)].reshape(keys, HD),
            preferred_element_type=jnp.float32,
        )
        done = (mixed / mass_ref[pair]).astype(jnp.bfloat16)
        for i in range(2):
            att_ref[0, :, head_lanes(2 * pair + i)] = done[i * tokens : (i + 1) * tokens]

    def mix_values():
        def one(step, carry):
            mix_pair(2 * step)
            mix_pair(2 * step + 1)
            return carry

        lax.fori_loop(0, heads // 4, one, 0)

    marks = [heads // 2 * part // 8 for part in split]
    loads[6].wait()
    loads[8].wait()
    for c in others:

        @pl.when(c < my_c)
        def _(c=c):
            ctx_copy(k_hbm.at[0], kbuf.at[c], k_send.at[c], k_recv.at[c], c).wait_recv()

    weigh(0, marks[0])

    def partial(c):
        block = arrived[c]
        if chunks > 1:
            block = jnp.dot(sort[...], block, preferred_element_type=jnp.float32).astype(
                jnp.bfloat16
            )
            block = jnp.concatenate(
                [block[j * rows_all : (j + 1) * rows_all] for j in range(chunks)], axis=1
            )
        return jnp.dot(block, wgu[...], preferred_element_type=jnp.float32)

    loads[4].wait()
    loads[5].wait()
    for c in others:
        group_of(arrived, a_send, a_recv, c, lines).wait_recv()
        rs_out[c] = partial(c).astype(jnp.bfloat16)
        ctx_copy(rs_out.at[c], rs_in.at[my_c], p_send.at[c], p_recv.at[my_c], c).start()
    group_of(arrived, a_send, a_recv, my_c, lines - message).wait_recv()
    own[...] = partial(my_c)
    loads[7].wait()
    loads[9].wait()
    weigh(marks[0], marks[1])
    for c in others:
        ctx_copy(rs_out.at[c], rs_in.at[c], p_send.at[c], p_recv.at[c], c).wait_recv()
    sums = own[...]
    for c in others:
        sums = sums + rs_in[c].astype(jnp.float32)
    gate = sums[:, :units]
    hid[my_c] = (gate / (1.0 + jnp.exp(-gate)) * sums[:, units:]).astype(jnp.bfloat16)
    for c in others:
        ctx_copy(hid.at[my_c], hid.at[my_c], h_send.at[c], h_recv.at[my_c], c).start()
    for c in others:

        @pl.when(c > my_c)
        def _(c=c):
            ctx_copy(v_hbm.at[0], vbuf.at[my_c], v_send.at[c], v_recv.at[my_c], c).start()


    def answer(c):
        block = jnp.dot(hid[c], wd_ref[...], preferred_element_type=jnp.float32).astype(
            jnp.bfloat16
        )
        if chunks > 1:
            block = jnp.concatenate(
                [block[:, j * wide : (j + 1) * wide] for j in range(chunks)], axis=0
            )
            block = jnp.dot(unsort[...], block, preferred_element_type=jnp.float32).astype(
                jnp.bfloat16
            )
        answers[c] = block

    answer(my_c)
    scatter(answers, ret, r_send, r_recv, my_c, n_dp - 1)
    ret[my_c, my_rows] = answers[my_c, my_rows]
    weigh(marks[1], heads // 2)
    for c in others:
        ctx_copy(hid.at[my_c], hid.at[c], h_send.at[c], h_recv.at[c], c).wait_recv()
        answer(c)
        scatter(answers, ret, r_send, r_recv, c, n_dp)
    for c in others:

        @pl.when(c < my_c)
        def _(c=c):
            ctx_copy(v_hbm.at[0], vbuf.at[c], v_send.at[c], v_recv.at[c], c).wait_recv()

    mix_values()

    def combine(c):
        part = ret[c]
        mixed = jnp.dot(w_back[...], part, preferred_element_type=jnp.float32)
        mixed = jnp.concatenate(
            [mixed[j * tokens : (j + 1) * tokens] for j in range(chunks)], axis=1
        )
        out_ref[0, :, pl.ds(pl.multiple_of(c * col, col), col)] = mixed.astype(jnp.bfloat16)

    group_of(ret, r_send, r_recv, my_c, lines - message).wait_recv()
    combine(my_c)
    for c in others:
        group_of(ret, r_send, r_recv, c, lines).wait_recv()
        combine(c)

    group_of(outgoing, a_send, a_recv, my_c, lines - message).wait_send()
    group_of(answers, r_send, r_recv, my_c, lines - message).wait_send()
    for c in others:

        @pl.when(c > my_c)
        def _(c=c):
            ctx_copy(k_hbm.at[0], kbuf.at[c], k_send.at[c], k_recv.at[c], c).wait_send()
            ctx_copy(v_hbm.at[0], vbuf.at[c], v_send.at[c], v_recv.at[c], c).wait_send()

        group_of(outgoing, a_send, a_recv, c, lines).wait_send()
        ctx_copy(rs_out.at[c], rs_in.at[c], p_send.at[c], p_recv.at[c], c).wait_send()
        ctx_copy(hid.at[my_c], hid.at[c], h_send.at[c], h_recv.at[c], c).wait_send()
        group_of(answers, r_send, r_recv, c, lines).wait_send()


def write_out(att_ref, out_ref, att_hbm, out_hbm, sems):
    copies = [
        pltpu.make_async_copy(att_ref, att_hbm, sems.at[0]),
        pltpu.make_async_copy(out_ref, out_hbm, sems.at[1]),
    ]
    for copy in copies:
        copy.start()
    for copy in copies:
        copy.wait()


def shards(
    n_ctx, n_dp, queries, key_rows, value_rows, stream, norm_gain, expert_ids, gate_values,
    w_gate, w_up, w_down,
):
    tokens, width = stream.shape[1:]
    top = expert_ids.shape[2]
    kv = key_rows.shape[2]
    units = w_gate.shape[2]
    col = width // n_ctx
    slot, chunks = message_form(col)
    rows = n_dp * slot
    lines = rows * chunks
    wide = col // chunks
    heads = queries.shape[2] // HD
    order = lines if chunks > 1 else TILE
    bf16, f32 = jnp.bfloat16, jnp.float32
    scratch = [
        ((tokens, queries.shape[2]), bf16),
        ((tokens, width), bf16),
        ((tokens, width), bf16),
        ((1, width), f32),
        ((top, tokens), jnp.int32),
        ((top, tokens), f32),
        ((col, 2 * units), bf16),
        ((units, col), bf16),
        ((n_ctx, lines, wide), bf16),
        ((n_ctx, lines, wide), bf16),
        ((n_ctx, tokens, kv), bf16),
        ((n_ctx, tokens, kv), bf16),
        ((n_ctx, rows, 2 * units), bf16),
        ((n_ctx, rows, 2 * units), bf16),
        ((rows, 2 * units), f32),
        ((n_ctx, rows, units), bf16),
        ((n_ctx, lines, wide), bf16),
        ((n_ctx, lines, wide), bf16),
        ((chunks * tokens, lines), bf16),
        ((tokens, n_ctx * tokens), f32),
        ((heads // 2, 2 * tokens, n_ctx * tokens), bf16),
        ((heads // 2, 2 * tokens, HD), f32),
        ((order, order), bf16),
        ((order, order), bf16),
    ]
    need = sum(math.prod(s) * jnp.dtype(t).itemsize for s, t in scratch)
    hbm = pl.BlockSpec(memory_space=pltpu.HBM)
    vmem = pl.BlockSpec(memory_space=pltpu.VMEM)
    operands = (
        queries, key_rows, value_rows, stream, norm_gain.reshape(1, width),
        expert_ids.swapaxes(1, 2), gate_values.swapaxes(1, 2), w_gate, w_up, w_down,
    )
    results = pl.pallas_call(
        functools.partial(fused, n_ctx, n_dp, (4, 6)),
        out_shape=(
            jax.ShapeDtypeStruct(queries.shape, bf16),
            jax.ShapeDtypeStruct(stream.shape, bf16),
        ),
        in_specs=[hbm] * 10,
        out_specs=(vmem, vmem),
        scratch_shapes=[pltpu.VMEM(s, t) for s, t in scratch]
        + [pltpu.SemaphoreType.DMA((n_ctx,))] * 12
        + [pltpu.SemaphoreType.DMA((10,))],
        compiler_params=pltpu.CompilerParams(
            collective_id=0, has_side_effects=True, vmem_limit_bytes=need + (16 << 20)
        ),
    )(*(pltpu.with_memory_space_constraint(x, pltpu.HBM) for x in operands))
    return pl.pallas_call(
        write_out,
        out_shape=tuple(jax.ShapeDtypeStruct(r.shape, r.dtype) for r in results),
        in_specs=[vmem, vmem],
        out_specs=(hbm, hbm),
        scratch_shapes=[pltpu.SemaphoreType.DMA((2,))],
        compiler_params=pltpu.CompilerParams(vmem_limit_bytes=8 << 20),
    )(*results)


def solution(mesh):
    rows = P("dp", "ctx", None)
    return jax.shard_map(
        functools.partial(shards, mesh.shape["ctx"], mesh.shape["dp"]),
        mesh=mesh,
        in_specs=(rows,) * 4 + (P(),) + (rows,) * 4 + (P("dp", None, "ctx"),),
        out_specs=(rows, rows),
        check_vma=False,
    )
```

```python
import functools
import math

import jax
import jax.numpy as jnp
from jax import lax
from jax.experimental import pallas as pl
from jax.experimental.pallas import tpu as pltpu
from jax.sharding import PartitionSpec as P

HD = 128
CAP = 12
TILE = 16
LANES = 128
MESH = pl.DeviceIdType.MESH
hidden_score = -1e30


def message_form(col):
    chunks = col // LANES
    if chunks * CAP % TILE == 0:
        return CAP, chunks
    return TILE, 1


def fused(
    n_ctx, n_dp,
    q_hbm, k_hbm, v_hbm, s_hbm, gain_hbm, ids_hbm, gv_hbm, wg_hbm, wu_hbm, wd_hbm,
    att_ref, out_ref,
    q_ref, s_ref, normed_ref, gain_ref, ids_ref, gv_ref, wgu, wd_ref,
    outgoing, arrived, kbuf, vbuf, rs_out, rs_in, own, hid, answers, ret,
    w_back, bias_ref, probs_ref, mass_ref, sort, unsort,
    k_send, k_recv, v_send, v_recv, a_send, a_recv, p_send, p_recv, h_send, h_recv,
    r_send, r_recv, load_sem,
):
    my_c = lax.axis_index("ctx")
    my_d = lax.axis_index("dp")
    me = my_c * n_dp + my_d
    total = n_ctx * n_dp
    tokens, width = s_ref.shape
    col = width // n_ctx
    slot, chunks = message_form(col)
    message = slot * chunks
    wide = col // chunks
    rows_all = n_dp * slot
    lines = n_dp * message
    units = wd_ref.shape[0]
    heads = q_ref.shape[1] // HD
    kv_heads = kbuf.shape[2] // HD
    group = heads // kv_heads

    pairs = (
        (ids_hbm.at[0], ids_ref),
        (gv_hbm.at[0], gv_ref),
        (s_hbm.at[0], s_ref),
        (gain_hbm, gain_ref),
        (wg_hbm.at[0], wgu.at[:, pl.ds(0, units)]),
        (wu_hbm.at[0], wgu.at[:, pl.ds(units, units)]),
        (k_hbm.at[0], kbuf.at[my_c]),
        (v_hbm.at[0], vbuf.at[my_c]),
        (q_hbm.at[0], q_ref),
        (wd_hbm.at[0], wd_ref),
    )
    loads = [pltpu.make_async_copy(a, b, load_sem.at[i]) for i, (a, b) in enumerate(pairs)]
    for load in loads:
        load.start()

    barrier = pltpu.get_barrier_semaphore()

    def greet(i, carry):
        peer = lax.rem(me + i, total)
        pl.semaphore_signal(
            barrier, inc=1, device_id=(peer // n_dp, lax.rem(peer, n_dp)), device_id_type=MESH
        )
        return carry

    lax.fori_loop(1, total, greet, 0)

    for c in range(1, n_ctx):

        @pl.when(c > my_c)
        def _(c=c):
            kbuf[c] = jnp.zeros_like(kbuf[c])
            vbuf[c] = jnp.zeros_like(vbuf[c])

    def whole_part(number, size):
        return jnp.floor((number + 0.5) * (1.0 / size))

    def parts_of(shape, dim):
        line = lax.broadcasted_iota(jnp.int32, shape, dim).astype(jnp.float32)
        owner = whole_part(line, message)
        rest = line - owner * message
        piece = whole_part(rest, slot)
        return owner, piece, rest - piece * slot

    expert, chunk, place_rank = parts_of((lines, 1), 0)
    expert_lane, chunk_lane, rank_lane = parts_of((1, lines), 1)
    expert_id = expert.astype(jnp.int32)
    loads[0].wait()
    loads[1].wait()
    hot = jnp.zeros((lines, tokens), jnp.float32)
    weight = jnp.zeros((lines, tokens), jnp.float32)
    for t in range(ids_ref.shape[0]):
        hit = ids_ref[t : t + 1, :] == expert_id
        hot = jnp.where(hit, 1.0, hot)
        weight = jnp.where(hit, gv_ref[t : t + 1, :], weight)
    rows_i = lax.broadcasted_iota(jnp.int32, (tokens, tokens), 0)
    cols_i = lax.broadcasted_iota(jnp.int32, (tokens, tokens), 1)
    before = jnp.where(rows_i < cols_i, 1.0, 0.0).astype(jnp.bfloat16)
    rank = jnp.dot(hot.astype(jnp.bfloat16), before, preferred_element_type=jnp.float32)
    place = jnp.where(rank == place_rank, hot, 0.0)
    select = jnp.concatenate(
        [jnp.where(chunk == j, place, 0.0).astype(jnp.bfloat16) for j in range(chunks)], axis=1
    )

    pl.semaphore_wait(barrier, total - 1)

    def ctx_copy(src, dst, send, recv, c):
        return pltpu.make_async_remote_copy(
            src_ref=src, dst_ref=dst, send_sem=send, recv_sem=recv,
            device_id=(c, my_d), device_id_type=MESH,
        )

    others = [lax.rem(my_c + i, n_ctx) for i in range(1, n_ctx)]
    my_rows = pl.ds(pl.multiple_of(my_d * message, message), message)

    half = n_dp // 2
    side = my_d // half

    def nth_peer(i):
        far = jnp.int32(i < half)
        step = lax.rem(my_d + i + 1 - far, half)
        return lax.rem(side + far, 2) * half + step

    def scatter(src, dst, send, recv, c, last):
        def one(i, carry):
            d = nth_peer(i)
            pltpu.make_async_remote_copy(
                src_ref=src.at[c, pl.ds(pl.multiple_of(d * message, message), message)],
                dst_ref=dst.at[my_c, my_rows],
                send_sem=send.at[c],
                recv_sem=recv.at[my_c],
                device_id=(c, d),
                device_id_type=MESH,
            ).start()
            return carry

        lax.fori_loop(0, last, one, 0, unroll=n_dp <= 8)

    def group_of(buf, send, recv, c, rows):
        part = buf.at[c, pl.ds(0, rows)]
        return pltpu.make_async_remote_copy(
            src_ref=part, dst_ref=part, send_sem=send.at[c], recv_sem=recv.at[c],
            device_id=(c, lax.rem(my_d + 1, n_dp)), device_id_type=MESH,
        )

    for c in others:

        @pl.when(c > my_c)
        def _(c=c):
            ctx_copy(k_hbm.at[0], kbuf.at[my_c], k_send.at[c], k_recv.at[my_c], c).start()


    loads[2].wait()
    loads[3].wait()
    x = s_ref[...].astype(jnp.float32)
    normed = (
        x * lax.rsqrt(jnp.mean(x * x, axis=-1, keepdims=True) + 1e-06) * gain_ref[...]
    ).astype(jnp.bfloat16)
    normed_ref[...] = normed
    for i, c in enumerate(others + [my_c]):
        stacked = jnp.concatenate(
            [
                normed_ref[:, pl.ds(pl.multiple_of(c * col + j * wide, wide), wide)]
                for j in range(chunks)
            ],
            axis=0,
        )
        outgoing[c] = jnp.dot(select, stacked, preferred_element_type=jnp.float32).astype(
            jnp.bfloat16
        )
        scatter(outgoing, arrived, a_send, a_recv, c, n_dp - 1 if i == n_ctx - 1 else n_dp)
    arrived[my_c, my_rows] = outgoing[my_c, my_rows]

    if chunks > 1:
        goes = (chunk * rows_all + expert * slot + place_rank).astype(jnp.int32)
        goes_lane = (chunk_lane * rows_all + expert_lane * slot + rank_lane).astype(jnp.int32)
        square = (lines, lines)
        unsort[...] = jnp.where(
            lax.broadcasted_iota(jnp.int32, square, 1) == goes, 1.0, 0.0
        ).astype(jnp.bfloat16)
        sort[...] = jnp.where(
            lax.broadcasted_iota(jnp.int32, square, 0) == goes_lane, 1.0, 0.0
        ).astype(jnp.bfloat16)

    back = (place * weight).T
    for j in range(chunks):
        w_back[j * tokens : (j + 1) * tokens] = jnp.where(chunk_lane == j, back, 0.0).astype(
            jnp.bfloat16
        )

    keys = n_ctx * tokens
    scale = math.log2(math.e) / math.sqrt(HD)
    q_pos = my_c * tokens + lax.broadcasted_iota(jnp.int32, (tokens, keys), 0)
    k_pos = lax.broadcasted_iota(jnp.int32, (tokens, keys), 1)
    bias_ref[...] = jnp.where(k_pos <= q_pos, 0.0, hidden_score)

    def kv_lanes(pair):
        return pl.ds(pl.multiple_of((2 * pair // group) * HD, HD), HD)

    def head_lanes(head):
        return pl.ds(pl.multiple_of(head * HD, HD), HD)

    def weigh(first, last):
        def one(pair, carry):
            two = jnp.concatenate([q_ref[:, head_lanes(2 * pair + i)] for i in range(2)], axis=0)
            scores = lax.dot_general(
                two, kbuf[:, :, kv_lanes(pair)].reshape(keys, HD), (((1,), (1,)), ((), ())),
                preferred_element_type=jnp.float32,
            ) * scale
            bias = bias_ref[...]
            scores = scores + jnp.concatenate([bias, bias], axis=0)
            probs = jnp.exp2(scores - jnp.max(scores, axis=-1, keepdims=True))
            mass = jnp.sum(probs, axis=-1, keepdims=True)
            probs_ref[pair] = probs.astype(jnp.bfloat16)
            mass_ref[pair] = jnp.broadcast_to(mass, (2 * tokens, HD))
            return carry

        lax.fori_loop(first, last, one, 0)

    def mix_pair(pair):
        mixed = jnp.dot(
            probs_ref[pair], vbuf[:, :, kv_lanes(pair)].reshape(keys, HD),
            preferred_element_type=jnp.float32,
        )
        done = (mixed / mass_ref[pair]).astype(jnp.bfloat16)
        for i in range(2):
            att_ref[0, :, head_lanes(2 * pair + i)] = done[i * tokens : (i + 1) * tokens]

    def mix_values():
        def one(step, carry):
            mix_pair(2 * step)
            mix_pair(2 * step + 1)
            return carry

        lax.fori_loop(0, heads // 4, one, 0)

    marks = [heads // 2 * i // n_ctx for i in range(n_ctx + 1)]
    loads[6].wait()
    loads[8].wait()
    for c in others:

        @pl.when(c < my_c)
        def _(c=c):
            ctx_copy(k_hbm.at[0], kbuf.at[c], k_send.at[c], k_recv.at[c], c).wait_recv()

    weigh(0, marks[1])

    def partial(c):
        block = arrived[c]
        if chunks > 1:
            block = jnp.dot(sort[...], block, preferred_element_type=jnp.float32).astype(
                jnp.bfloat16
            )
            block = jnp.concatenate(
                [block[j * rows_all : (j + 1) * rows_all] for j in range(chunks)], axis=1
            )
        return jnp.dot(block, wgu[...], preferred_element_type=jnp.float32)

    loads[4].wait()
    loads[5].wait()
    for i, c in enumerate(others):
        group_of(arrived, a_send, a_recv, c, lines).wait_recv()
        rs_out[c] = partial(c).astype(jnp.bfloat16)
        ctx_copy(rs_out.at[c], rs_in.at[my_c], p_send.at[c], p_recv.at[my_c], c).start()
        weigh(marks[i + 1], marks[i + 2])
    group_of(arrived, a_send, a_recv, my_c, lines - message).wait_recv()
    own[...] = partial(my_c)
    loads[7].wait()
    loads[9].wait()
    for c in others:
        ctx_copy(rs_out.at[c], rs_in.at[c], p_send.at[c], p_recv.at[c], c).wait_recv()
    sums = own[...]
    for c in others:
        sums = sums + rs_in[c].astype(jnp.float32)
    gate = sums[:, :units]
    hid[my_c] = (gate / (1.0 + jnp.exp(-gate)) * sums[:, units:]).astype(jnp.bfloat16)
    for c in others:
        ctx_copy(hid.at[my_c], hid.at[my_c], h_send.at[c], h_recv.at[my_c], c).start()
    for c in others:

        @pl.when(c > my_c)
        def _(c=c):
            ctx_copy(v_hbm.at[0], vbuf.at[my_c], v_send.at[c], v_recv.at[my_c], c).start()


    def answer(c):
        block = jnp.dot(hid[c], wd_ref[...], preferred_element_type=jnp.float32).astype(
            jnp.bfloat16
        )
        if chunks > 1:
            block = jnp.concatenate(
                [block[:, j * wide : (j + 1) * wide] for j in range(chunks)], axis=0
            )
            block = jnp.dot(unsort[...], block, preferred_element_type=jnp.float32).astype(
                jnp.bfloat16
            )
        answers[c] = block

    answer(my_c)
    scatter(answers, ret, r_send, r_recv, my_c, n_dp - 1)
    ret[my_c, my_rows] = answers[my_c, my_rows]
    for c in others:
        ctx_copy(hid.at[my_c], hid.at[c], h_send.at[c], h_recv.at[c], c).wait_recv()
        answer(c)
        scatter(answers, ret, r_send, r_recv, c, n_dp)
    for c in others:

        @pl.when(c < my_c)
        def _(c=c):
            ctx_copy(v_hbm.at[0], vbuf.at[c], v_send.at[c], v_recv.at[c], c).wait_recv()

    mix_values()

    def combine(c):
        part = ret[c]
        mixed = jnp.dot(w_back[...], part, preferred_element_type=jnp.float32)
        mixed = jnp.concatenate(
            [mixed[j * tokens : (j + 1) * tokens] for j in range(chunks)], axis=1
        )
        out_ref[0, :, pl.ds(pl.multiple_of(c * col, col), col)] = mixed.astype(jnp.bfloat16)

    group_of(ret, r_send, r_recv, my_c, lines - message).wait_recv()
    combine(my_c)
    for c in others:
        group_of(ret, r_send, r_recv, c, lines).wait_recv()
        combine(c)

    group_of(outgoing, a_send, a_recv, my_c, lines - message).wait_send()
    group_of(answers, r_send, r_recv, my_c, lines - message).wait_send()
    for c in others:

        @pl.when(c > my_c)
        def _(c=c):
            ctx_copy(k_hbm.at[0], kbuf.at[c], k_send.at[c], k_recv.at[c], c).wait_send()
            ctx_copy(v_hbm.at[0], vbuf.at[c], v_send.at[c], v_recv.at[c], c).wait_send()

        group_of(outgoing, a_send, a_recv, c, lines).wait_send()
        ctx_copy(rs_out.at[c], rs_in.at[c], p_send.at[c], p_recv.at[c], c).wait_send()
        ctx_copy(hid.at[my_c], hid.at[c], h_send.at[c], h_recv.at[c], c).wait_send()
        group_of(answers, r_send, r_recv, c, lines).wait_send()


def write_out(att_ref, out_ref, att_hbm, out_hbm, sems):
    copies = [
        pltpu.make_async_copy(att_ref, att_hbm, sems.at[0]),
        pltpu.make_async_copy(out_ref, out_hbm, sems.at[1]),
    ]
    for copy in copies:
        copy.start()
    for copy in copies:
        copy.wait()


def shards(
    n_ctx, n_dp, queries, key_rows, value_rows, stream, norm_gain, expert_ids, gate_values,
    w_gate, w_up, w_down,
):
    tokens, width = stream.shape[1:]
    top = expert_ids.shape[2]
    kv = key_rows.shape[2]
    units = w_gate.shape[2]
    col = width // n_ctx
    slot, chunks = message_form(col)
    rows = n_dp * slot
    lines = rows * chunks
    wide = col // chunks
    heads = queries.shape[2] // HD
    order = lines if chunks > 1 else TILE
    bf16, f32 = jnp.bfloat16, jnp.float32
    scratch = [
        ((tokens, queries.shape[2]), bf16),
        ((tokens, width), bf16),
        ((tokens, width), bf16),
        ((1, width), f32),
        ((top, tokens), jnp.int32),
        ((top, tokens), f32),
        ((col, 2 * units), bf16),
        ((units, col), bf16),
        ((n_ctx, lines, wide), bf16),
        ((n_ctx, lines, wide), bf16),
        ((n_ctx, tokens, kv), bf16),
        ((n_ctx, tokens, kv), bf16),
        ((n_ctx, rows, 2 * units), bf16),
        ((n_ctx, rows, 2 * units), bf16),
        ((rows, 2 * units), f32),
        ((n_ctx, rows, units), bf16),
        ((n_ctx, lines, wide), bf16),
        ((n_ctx, lines, wide), bf16),
        ((chunks * tokens, lines), bf16),
        ((tokens, n_ctx * tokens), f32),
        ((heads // 2, 2 * tokens, n_ctx * tokens), bf16),
        ((heads // 2, 2 * tokens, HD), f32),
        ((order, order), bf16),
        ((order, order), bf16),
    ]
    need = sum(math.prod(s) * jnp.dtype(t).itemsize for s, t in scratch)
    hbm = pl.BlockSpec(memory_space=pltpu.HBM)
    vmem = pl.BlockSpec(memory_space=pltpu.VMEM)
    operands = (
        queries, key_rows, value_rows, stream, norm_gain.reshape(1, width),
        expert_ids.swapaxes(1, 2), gate_values.swapaxes(1, 2), w_gate, w_up, w_down,
    )
    results = pl.pallas_call(
        functools.partial(fused, n_ctx, n_dp),
        out_shape=(
            jax.ShapeDtypeStruct(queries.shape, bf16),
            jax.ShapeDtypeStruct(stream.shape, bf16),
        ),
        in_specs=[hbm] * 10,
        out_specs=(vmem, vmem),
        scratch_shapes=[pltpu.VMEM(s, t) for s, t in scratch]
        + [pltpu.SemaphoreType.DMA((n_ctx,))] * 12
        + [pltpu.SemaphoreType.DMA((10,))],
        compiler_params=pltpu.CompilerParams(
            collective_id=0, has_side_effects=True, vmem_limit_bytes=need + (16 << 20)
        ),
    )(*(pltpu.with_memory_space_constraint(x, pltpu.HBM) for x in operands))
    return pl.pallas_call(
        write_out,
        out_shape=tuple(jax.ShapeDtypeStruct(r.shape, r.dtype) for r in results),
        in_specs=[vmem, vmem],
        out_specs=(hbm, hbm),
        scratch_shapes=[pltpu.SemaphoreType.DMA((2,))],
        compiler_params=pltpu.CompilerParams(vmem_limit_bytes=8 << 20),
    )(*results)


def solution(mesh):
    rows = P("dp", "ctx", None)
    return jax.shard_map(
        functools.partial(shards, mesh.shape["ctx"], mesh.shape["dp"]),
        mesh=mesh,
        in_specs=(rows,) * 4 + (P(),) + (rows,) * 4 + (P("dp", None, "ctx"),),
        out_specs=(rows, rows),
        check_vma=False,
    )
```
